256 devices in a mesh: blk: 64 (over y, z_hi, x, core), rep: 4 (over z_lo).
Axes of the slice: x: 4, y: 4, z: 8 (z_hi: 2, z_lo: 4; z = z_hi * 4 + z_lo), core: 2. Of those that a mesh axis runs over, the one named last changes fastest.
Arguments:
- factors_in: float32 [16384, 256], P('blk', 'rep'), may hold values from -6 to 6
- items: float32 [8192, 256], P('blk', 'rep'), may hold values from -0.0625 to 0.0625
- tile_user: int32 [64, 128], P('blk', 'rep'), may hold values from 0 to 1
- levels: int32 [64, 128, 128, 128], P('blk', 'rep'), may hold values from 0 to 15
Outputs:
- factors: float32 [16384, 256], P('blk', 'rep')
- item_rhs: float32 [8192, 256], P('blk', 'rep')
The draws below stay inside these ranges and needn't reach their ends.
All inputs are finite; a program needn't handle non-finite values.
Results may differ from the reference program's by a relative error of at most 0.0003.
Values sent between devices are 32-bit elements; how exact they have to be, the bound alone decides.
No kernel may reach another device: no remote copies, remote signals or barrier semaphores. Data moves between devices by JAX's collectives and lax.ppermute only.
A program may use at most 128 MiB of HBM per device.

```python
import jax
import jax.numpy as jnp
from jax import lax

R = 256
TILE = 128
U_DEV = 256
ITERS = 2
USERS = 16384
ITEMS = 8192
TILES = 128
N_BLK = 64
N_REP = 4


def plant(values, rng, low, largest):
    dims = values.shape
    index_at = [jax.random.randint(jax.random.fold_in(rng, axis), (), 0, dims[axis]) for axis in range(len(dims))]
    values = values.at[tuple(index_at)].set(low)
    longest = dims.index(max(dims))
    index_at[longest] = (index_at[longest] + 1) % dims[longest]
    return values.at[tuple(index_at)].set(largest)


def shard_levels(stream_key, shape, split, low, top_value):
    def one(position, parts):
        heights = jax.random.uniform(jax.random.fold_in(jax.random.fold_in(stream_key, 6), position), (parts,), jnp.float32, low / len(split), top_value / len(split))
        return jnp.repeat(jnp.exp(heights), shape[position] // parts).reshape((-1,) + (1,) * (len(shape) - position - 1))

    gain = one(*split[0])
    for cut in split[1:]:
        gain = gain * one(*cut)
    return gain


def bell_draw(key, dims, deviation, most, cuts=(), kind=jnp.bfloat16):
    values = deviation * jax.random.normal(key, dims, jnp.float32)
    if cuts:
        values = values * shard_levels(key, dims, cuts, -0.22, 0.18)
    return jnp.clip(values, -most, most).astype(kind)


def setup_inputs(seed: int = 0) -> dict:
    keys = jax.random.split(jax.random.key(seed), 5)
    return {
        "factors_in": bell_draw(keys[0], (USERS, R), 1.0, 6.0, ((0, 64), (1, 4)), jnp.float32),
        "items": bell_draw(keys[1], (ITEMS, R), (TILE * N_BLK) ** -0.5, 0.0625, ((0, 64), (1, 4)), jnp.float32),
        "tile_user": plant(jax.random.randint(keys[2], (N_BLK, TILES), 0, U_DEV // TILE), jax.random.fold_in(keys[2], 1), 0, (U_DEV // TILE) - 1).astype(jnp.int32),
        "levels": plant(jax.random.randint(keys[3], (N_BLK, TILES, TILE, TILE), 0, 16), jax.random.fold_in(keys[3], 1), 0, 15).astype(jnp.int32),
    }


precise = lax.Precision.HIGHEST
conf_scale = 0.1
ridge_term = 0.1


def reference(factors_in, items, tile_user, levels):
    blocks = U_DEV // TILE
    gram = jnp.dot(items.T, items, precision=precise, preferred_element_type=jnp.float32)
    shifted = gram + ridge_term * jnp.eye(R, dtype=jnp.float32)
    panels = jnp.tile(items.reshape(N_BLK, TILE, R), (N_REP // 2, 1, 1))
    columns = jnp.arange(blocks, dtype=jnp.int32)
    starts = jnp.arange(N_BLK, dtype=jnp.int32) * U_DEV

    def shard_step(item_total, inputs):
        start_rows, users, lev = inputs
        weight = conf_scale * lev.astype(jnp.float32)
        target = jnp.where(lev > 0, 1.0 + weight, 0.0)
        onehot = (users[:, None] == columns[None, :]).astype(jnp.float32)

        def pick(vectors):
            return jnp.take(vectors.reshape(blocks, TILE, R), users, axis=0)

        def spread(terms):
            return jnp.einsum("nb,ntr->btr", onehot, terms, precision=precise).reshape(U_DEV, R)

        def scores(vectors):
            return jnp.einsum("ntr,nir->nti", pick(vectors), panels, precision=precise)

        def project(mixed):
            return jnp.einsum("nti,nir->ntr", mixed, panels, precision=precise)

        start_x = lax.dynamic_slice_in_dim(factors_in, start_rows, U_DEV, 0)
        resid = spread(project(target - weight * scores(start_x))) - jnp.dot(start_x, shifted, precision=precise, preferred_element_type=jnp.float32)
        solution = start_x
        direc = resid
        rho = jnp.sum(resid * resid, axis=1, keepdims=True)
        for step in range(ITERS):
            image = spread(project(weight * scores(direc))) + jnp.dot(direc, shifted, precision=precise, preferred_element_type=jnp.float32)
            alpha = rho / jnp.sum(direc * image, axis=1, keepdims=True)
            solution = solution + alpha * direc
            resid = resid - alpha * image
            rho_next = jnp.sum(resid * resid, axis=1, keepdims=True)
            direc = resid + (rho_next / rho) * direc
            rho = rho_next
        term = jnp.einsum("nti,ntr->nir", target, pick(solution), precision=precise)
        item_total = item_total + jnp.sum(term.reshape(N_REP // 2, N_BLK * TILE, R), axis=0)
        return item_total, solution

    init = jnp.zeros((N_BLK * TILE, R), jnp.float32)
    item_total, solved = lax.scan(shard_step, init, (starts, tile_user, levels))
    scale = ((N_REP // 2) * N_BLK * TILE) ** -0.5
    return solved.reshape(N_BLK * U_DEV, R), item_total * scale
```

```python
import functools

import jax
import jax.numpy as jnp
import numpy as np
from jax import lax
from jax.experimental import pallas as pl
from jax.experimental.pallas import tpu as pltpu
from jax.sharding import Mesh, PartitionSpec as P

ITERS = 2
AXES = ("y", "zh", "x", "core", "rep")
SIZES = (4, 2, 4, 2, 4)
BLK = ("y", "zh", "x", "core")
RANK = 256
TILE = 128
HALF = TILE // 2
GROUPS = 8
WIDE = 4 * TILE
RIDGE = 0.1
STEP = 0.1
VMEM = 48 * 1024 * 1024
f32 = jnp.float32
bf16 = jnp.bfloat16


def split(value):
    high = value.astype(bf16)
    low = (value - high.astype(f32)).astype(bf16)
    return high, low


def dot(a, b):
    return lax.dot_general(a, b, (((1,), (0,)), ((), ())), preferred_element_type=f32)


def dot_t(a, b):
    return lax.dot_general(a, b, (((1,), (1,)), ((), ())), preferred_element_type=f32)


def scores_of(stacked, panel_hi, panel_lo):
    both = dot(stacked, panel_hi)
    return both[:TILE] + both[TILE:] + dot(stacked[:TILE], panel_lo)


def project(mixed, panel_hi, panel_lo):
    high, low = split(mixed)
    both = dot_t(jnp.concatenate([high, low], axis=0), panel_hi)
    return both[:TILE] + both[TILE:] + dot_t(high, panel_lo)


def store_split(vectors, stacked):
    high, low = split(vectors)
    stacked[:TILE] = high
    stacked[TILE:] = low


def first_kernel(scal, x0, panels, lev_a, lev_b, hi, lo, weight, target, part, stacked):
    i = pl.program_id(0)

    @pl.when(i == 0)
    def _():
        store_split(x0[...], stacked)
        part[...] = jnp.zeros_like(part)

    for j in range(4):
        cols = slice(j * TILE, (j + 1) * TILE)
        tile = j * GROUPS + i
        a1 = scal[1 + tile].astype(f32)
        b1 = scal[33 + tile].astype(f32)
        a0, b0 = 1.0 - a1, 1.0 - b1
        la = lev_a[j, 0, 0].astype(f32)
        lb = lev_b[j, 0].astype(f32)
        ta = la + jnp.where(la > 0, 10.0, 0.0)
        tb = lb + jnp.where(lb > 0, 10.0, 0.0)
        weight[0, :HALF, cols] = (10.0 + a0 * la + b0 * lb).astype(bf16)
        weight[0, HALF:, cols] = (10.0 + a1 * la + b1 * lb).astype(bf16)
        target[0, :HALF, cols] = a0 * ta + b0 * tb
        target[0, HALF:, cols] = a1 * ta + b1 * tb
        high, low = split(panels[0, j])
        hi[0, :, cols] = high
        lo[0, :, cols] = low
    scores = scores_of(stacked[...], hi[0], lo[0])
    mixed = STEP * (target[0] - weight[0].astype(f32) * scores)
    part[...] += project(mixed, hi[0], lo[0])


def apply_step(hi, lo, weight, part, stacked):
    scores = scores_of(stacked[...], hi[0], lo[0])
    mixed = STEP * (weight[0].astype(f32) * scores)
    part[...] += project(mixed, hi[0], lo[0])


def second_kernel(pa, pb, x0, hi, lo, weight, resid, part, stacked):
    @pl.when(pl.program_id(0) == 0)
    def _():
        start = pa[...] + pb[...] - RIDGE * x0[...]
        resid[...] = start
        store_split(start, stacked)
        part[...] = jnp.zeros_like(part)

    apply_step(hi, lo, weight, part, stacked)


def third_kernel(pa, pb, resid, x0, hi, lo, weight, x1, resid1, direc1, part, stacked):
    @pl.when(pl.program_id(0) == 0)
    def _():
        direc = resid[...]
        image = pa[...] + pb[...] + RIDGE * direc
        rho = jnp.sum(direc * direc, axis=1, keepdims=True)
        alpha = rho / jnp.sum(direc * image, axis=1, keepdims=True)
        x1[...] = x0[...] + alpha * direc
        after = direc - alpha * image
        resid1[...] = after
        rho_next = jnp.sum(after * after, axis=1, keepdims=True)
        ahead = after + (rho_next / rho) * direc
        direc1[...] = ahead
        store_split(ahead, stacked)
        part[...] = jnp.zeros_like(part)

    apply_step(hi, lo, weight, part, stacked)


def last_kernel(pa, pb, resid, direc, x1, out):
    image = pa[...] + pb[...] + RIDGE * direc[...]
    rho = jnp.sum(resid[...] * resid[...], axis=1, keepdims=True)
    alpha = rho / jnp.sum(direc[...] * image, axis=1, keepdims=True)
    out[...] = x1[...] + alpha * direc[...]


def rhs_kernel(scal, vectors, own, got, t1, t2, t3, out, total):
    x, core = scal[0], scal[1]
    for k in range(4):
        source = lax.rem(x + 4 - k, 4)
        for slot in range(2):
            src_core = core if slot == 0 else 1 - core
            chunk = vectors[source * 2 + src_core]
            if k == 0:
                tile = (own, got)[slot][x]
            else:
                tile = (t1, t2, t3)[k - 1][slot]
            tile = tile.astype(bf16)
            high, low = split(chunk.T)
            both = jnp.concatenate([high, low], axis=1)
            term = dot(both, jnp.concatenate([tile, tile], axis=0))
            if k == 0 and slot == 0:
                total[...] = term
            else:
                total[...] += term
    for j in range(4):
        out[j] = total[:, j * TILE : (j + 1) * TILE]


def spec(shape, index=None):
    if index is None:
        zeros = (0,) * len(shape)
        return pl.BlockSpec(shape, lambda *_: zeros)
    return pl.BlockSpec(shape, index)


def params():
    return pltpu.CompilerParams(vmem_limit_bytes=VMEM)


def cost(flops, moved):
    return pl.CostEstimate(flops=flops, bytes_accessed=moved, transcendentals=0)


APPLY_COST = 6 * 2 * TILE * GROUPS * WIDE * RANK


def panel_specs():
    return [
        spec((1, RANK, WIDE), lambda i, *_: (i, 0, 0)),
        spec((1, RANK, WIDE), lambda i, *_: (i, 0, 0)),
        spec((1, TILE, WIDE), lambda i, *_: (i, 0, 0)),
    ]


def shaped(*shape, dtype=f32):
    return jax.ShapeDtypeStruct(shape, dtype)


def first_apply(scal, x0, panels, lev_a, lev_b):
    whole = (TILE, RANK)
    return pl.pallas_call(
        first_kernel,
        grid_spec=pltpu.PrefetchScalarGridSpec(
            num_scalar_prefetch=1,
            grid=(GROUPS,),
            in_specs=[
                spec(whole),
                spec((1, 4, RANK, TILE), lambda i, s: (i, 0, 0, 0)),
                spec((4, 1, 1, HALF, TILE), lambda i, s: (0, i, s[0], 0, 0)),
                spec((4, 1, HALF, TILE), lambda i, s: (0, i, 0, 0)),
            ],
            out_specs=panel_specs()
            + [spec((1, TILE, WIDE), lambda i, s: (i, 0, 0)), spec(whole)],
            scratch_shapes=[pltpu.VMEM((2 * TILE, RANK), bf16)],
        ),
        out_shape=[
            shaped(GROUPS, RANK, WIDE, dtype=bf16),
            shaped(GROUPS, RANK, WIDE, dtype=bf16),
            shaped(GROUPS, TILE, WIDE, dtype=bf16),
            shaped(GROUPS, TILE, WIDE),
            shaped(*whole),
        ],
        compiler_params=params(),
        cost_estimate=cost(APPLY_COST, 14 << 20),
        name="first_apply",
    )(scal, x0, panels, lev_a, lev_b)


def next_apply(kernel, vectors, panels, outs, name):
    whole = (TILE, RANK)
    return pl.pallas_call(
        kernel,
        grid=(GROUPS,),
        in_specs=[spec(whole)] * len(vectors) + panel_specs(),
        out_specs=[spec(whole)] * outs,
        out_shape=[shaped(*whole)] * outs,
        scratch_shapes=[pltpu.VMEM((2 * TILE, RANK), bf16)],
        compiler_params=params(),
        cost_estimate=cost(APPLY_COST, 6 << 20),
        name=name,
    )(*vectors, *panels)


def shift(value, axis, size, by):
    return lax.ppermute(value, axis, [(i, (i + by) % size) for i in range(size)])


def flip(value, axis, size, bit):
    return lax.ppermute(value, axis, [(i, i ^ bit) for i in range(size)])


def pick(value, index, axis=0):
    return lax.dynamic_index_in_dim(value, index, axis, keepdims=False)


def per_device(factors_in, items, tile_user, levels):
    y, zh, x, core, rep = (lax.axis_index(name) for name in AXES)
    half, parity = rep // 2, rep % 2
    strip = RANK // 4

    packed = jnp.concatenate(
        [items.T[None], factors_in.T.reshape(strip, 2, TILE).transpose(1, 0, 2)], axis=0
    )
    column = lax.all_gather(packed, ("zh", "rep"), axis=0, tiled=False)
    lev = levels[0].reshape(32, 2, HALF, TILE)
    other = pick(lev, 1 - half, 1)
    other, column = lax.optimization_barrier((other, column))
    lev_b = flip(other, "rep", 4, 2)
    user_b = flip(tile_user, "rep", 4, 2)
    scal = jnp.concatenate([half[None].astype(jnp.int32), tile_user[0], user_b[0]])

    mine = lax.dynamic_slice(column, (zh * 4, 1, 0, half * HALF), (4, 2, strip, HALF))
    x0 = mine.transpose(1, 3, 0, 2).reshape(TILE, RANK)

    panel = column[:, 0].reshape(2, RANK, TILE)
    panel = lax.all_gather(panel, "y", axis=0, tiled=False)
    panel = lax.dynamic_slice_in_dim(panel, 2 * parity, 2, 0).reshape(4, RANK, TILE)
    panels = lax.all_gather(panel, ("x", "core"), axis=0, tiled=False)

    hi, lo, weight, target, part = first_apply(
        scal,
        x0,
        panels,
        lev.reshape(4, GROUPS, 2, HALF, TILE),
        lev_b.reshape(4, GROUPS, HALF, TILE),
    )
    shared = (hi, lo, weight)
    part_b = flip(part, "rep", 4, 1)

    target = target.reshape(4, 2, TILE, WIDE)
    own = pick(target, core, 1)
    got = flip(pick(target, 1 - core, 1), "core", 2, 1)
    moved = []
    for k in (1, 2, 3):
        to = (x + k) % 4
        moved.append(shift(jnp.stack([pick(own, to), pick(got, to)]), "x", 4, k))

    resid, part = next_apply(second_kernel, (part, part_b, x0), shared, 2, "second_apply")
    part_b = flip(part, "rep", 4, 1)
    x1, resid1, direc1, part = next_apply(
        third_kernel, (part, part_b, resid, x0), shared, 4, "third_apply"
    )
    part_b = flip(part, "rep", 4, 1)
    solved = pl.pallas_call(
        last_kernel,
        out_shape=shaped(TILE, RANK),
        compiler_params=params(),
        cost_estimate=cost(TILE * RANK * 10, 6 * TILE * RANK * 4),
        name="last_update",
    )(part, part_b, resid1, direc1, x1)

    vectors = lax.all_gather(solved, ("x", "core"), axis=0, tiled=False)

    strips = solved.reshape(TILE, 4, strip)
    sent = flip(pick(strips, rep ^ 2, 1), "rep", 4, 2)
    kept = pick(strips, rep, 1)
    low = jnp.where(half == 0, kept, sent).reshape(2, HALF, strip)
    high = jnp.where(half == 0, sent, kept).reshape(2, HALF, strip)
    factors = jnp.stack([low, high], axis=1).reshape(2 * TILE, strip)

    smem = pl.BlockSpec(memory_space=pltpu.SMEM)
    vmem = pl.BlockSpec(memory_space=pltpu.VMEM)
    terms = pl.pallas_call(
        rhs_kernel,
        in_specs=[smem] + [vmem] * 6,
        out_shape=shaped(4, RANK, TILE),
        scratch_shapes=[pltpu.VMEM((RANK, WIDE), f32)],
        compiler_params=params(),
        cost_estimate=cost(4 * 1024 * RANK * WIDE, 4 << 20),
        name="rhs_terms",
    )(jnp.stack([x, core]).astype(jnp.int32), vectors, own, got, *moved)

    terms = terms.reshape(2, 2 * RANK, TILE)
    near, far = pick(terms, y % 2), pick(terms, 1 - y % 2)

    def along_y(value, move, inside):
        pairs = [
            (s * 4 + r, move(s) * 4 + r)
            for s in range(4)
            for r in range(4)
            if (s // 2 == r % 2) == inside
        ]
        return lax.ppermute(value, ("y", "rep"), pairs)

    summed = (
        near
        + along_y(far, lambda s: s ^ 1, True)
        + along_y(far, lambda s: 3 - s, False)
        + along_y(near, lambda s: (s + 2) % 4, False)
    )
    pieces = lax.all_to_all(
        summed.reshape(8, strip, TILE), ("zh", "rep"), split_axis=0, concat_axis=0, tiled=True
    )
    chosen = pick(pieces.reshape(2, 2, 2, strip, TILE), y // 2, 2)
    scale = (2 * 64 * TILE) ** -0.5
    item_rhs = jnp.sum(chosen, axis=(0, 1)).T * (scale * STEP)
    return factors, item_rhs


def solution(mesh):
    fine = Mesh(np.asarray(mesh.devices).reshape(SIZES), AXES)
    rows = P(BLK, "rep")
    return jax.shard_map(
        per_device,
        mesh=fine,
        in_specs=(rows, rows, rows, P(BLK, "rep", None, None)),
        out_specs=(rows, rows),
        check_vma=False,
    )
```

```python
import functools

import jax
import jax.numpy as jnp
import numpy as np
from jax import lax
from jax.experimental import pallas as pl
from jax.experimental.pallas import tpu as pltpu
from jax.sharding import Mesh, PartitionSpec as P

ITERS = 2
AXES = ("y", "zh", "x", "core", "rep")
SIZES = (4, 2, 4, 2, 4)
BLK = ("y", "zh", "x", "core")
RANK = 256
TILE = 128
HALF = TILE // 2
GROUPS = 8
WIDE = 4 * TILE
RIDGE = 0.1
STEP = 0.1
f32 = jnp.float32
bf16 = jnp.bfloat16


def split(value):
    high = value.astype(bf16)
    low = (value - high.astype(f32)).astype(bf16)
    return high, low


def dot(a, b):
    return lax.dot_general(a, b, (((1,), (0,)), ((), ())), preferred_element_type=f32)


def dot_t(a, b):
    return lax.dot_general(a, b, (((1,), (1,)), ((), ())), preferred_element_type=f32)


def scores_of(stacked, panel_hi, panel_lo):
    both = dot(stacked, panel_hi)
    return both[:TILE] + both[TILE:] + dot(stacked[:TILE], panel_lo)


def project(mixed, panel_hi, panel_lo):
    high, low = split(mixed)
    both = dot_t(jnp.concatenate([high, low], axis=0), panel_hi)
    return both[:TILE] + both[TILE:] + dot_t(high, panel_lo)


def store_split(vectors, stacked):
    high, low = split(vectors)
    stacked[:TILE] = high
    stacked[TILE:] = low


def scores_kernel(
    x0_t, own, far, own_hi, own_lo, far_hi, far_lo, own_scores, far_scores, x0, stacked
):
    @pl.when(pl.program_id(0) == 0)
    def _():
        start = x0_t[...].T
        x0[...] = start
        store_split(start, stacked)

    sides = ((own, own_hi, own_lo, own_scores), (far, far_hi, far_lo, far_scores))
    for panels, hi, lo, scores in sides:
        for j in range(4):
            cols = slice(j * TILE, (j + 1) * TILE)
            high, low = split(panels[0, j])
            hi[0, :, cols] = high
            lo[0, :, cols] = low
        scores[0] = scores_of(stacked[...], hi[0], lo[0])


def first_kernel(scal, *refs):
    (
        own_scores, far_scores, own_hi, own_lo, far_hi, far_lo,
        own_a, own_b, own_c, own_d, far_a, far_b, far_c, far_d,
        own_weight, far_weight, own_target, far_target, part,
    ) = refs
    i = pl.program_id(0)
    core = scal[1]

    @pl.when(i == 0)
    def _():
        part[...] = jnp.zeros_like(part)

    sides = (
        (core, own_scores, own_hi, own_lo, own_a, (own_b, own_c, own_d), own_weight, own_target),
        (1 - core, far_scores, far_hi, far_lo, far_a, (far_b, far_c, far_d), far_weight, far_target),
    )
    for which, scores, hi, lo, lev_a, moved, weight, target in sides:
        for j in range(4):
            cols = slice(j * TILE, (j + 1) * TILE)
            tile = j * GROUPS + i * 2 + which
            a1 = scal[2 + tile].astype(f32)
            b1 = scal[34 + tile].astype(f32)
            a0, b0 = 1.0 - a1, 1.0 - b1
            la = lev_a[j, 0, 0].astype(f32)
            lb = moved[min(j, 2)][max(j - 2, 0), 0].astype(f32)
            ta = la + jnp.where(la > 0, 10.0, 0.0)
            tb = lb + jnp.where(lb > 0, 10.0, 0.0)
            weight[0, :HALF, cols] = (10.0 + a0 * la + b0 * lb).astype(bf16)
            weight[0, HALF:, cols] = (10.0 + a1 * la + b1 * lb).astype(bf16)
            target[0, :HALF, cols] = a0 * ta + b0 * tb
            target[0, HALF:, cols] = a1 * ta + b1 * tb
        mixed = STEP * (target[0] - weight[0].astype(f32) * scores[0])
        part[...] += project(mixed, hi[0], lo[0])


def apply_step(shared, part, stacked):
    own_hi, own_lo, far_hi, far_lo, own_weight, far_weight = shared
    for hi, lo, weight in ((own_hi, own_lo, own_weight), (far_hi, far_lo, far_weight)):
        scores = scores_of(stacked[...], hi[0], lo[0])
        mixed = STEP * (weight[0].astype(f32) * scores)
        part[...] += project(mixed, hi[0], lo[0])


def second_kernel(pa, pb, x0, *refs):
    shared, (resid, part, stacked) = refs[:6], refs[6:]

    @pl.when(pl.program_id(0) == 0)
    def _():
        start = pa[...] + pb[...] - RIDGE * x0[...]
        resid[...] = start
        store_split(start, stacked)
        part[...] = jnp.zeros_like(part)

    apply_step(shared, part, stacked)


def third_kernel(pa, pb, resid, x0, *refs):
    shared, (x1, resid1, direc1, part, stacked) = refs[:6], refs[6:]

    @pl.when(pl.program_id(0) == 0)
    def _():
        direc = resid[...]
        image = pa[...] + pb[...] + RIDGE * direc
        rho = jnp.sum(direc * direc, axis=1, keepdims=True)
        alpha = rho / jnp.sum(direc * image, axis=1, keepdims=True)
        x1[...] = x0[...] + alpha * direc
        after = direc - alpha * image
        resid1[...] = after
        rho_next = jnp.sum(after * after, axis=1, keepdims=True)
        ahead = after + (rho_next / rho) * direc
        direc1[...] = ahead
        store_split(ahead, stacked)
        part[...] = jnp.zeros_like(part)

    apply_step(shared, part, stacked)


def last_kernel(pa, pb, resid, direc, x1, out):
    image = pa[...] + pb[...] + RIDGE * direc[...]
    rho = jnp.sum(resid[...] * resid[...], axis=1, keepdims=True)
    alpha = rho / jnp.sum(direc[...] * image, axis=1, keepdims=True)
    out[...] = x1[...] + alpha * direc[...]


def rhs_kernel(scal, vectors, own, got, t1, t2, t3, out, total):
    x = scal[0]
    for k in range(4):
        source = lax.rem(x + 4 - k, 4)
        for slot in range(2):
            chunk = vectors[source, slot]
            if k == 0:
                tile = (own, got)[slot][x]
            else:
                tile = (t1, t2, t3)[k - 1][slot]
            tile = tile.astype(bf16)
            high, low = split(chunk.T)
            both = jnp.concatenate([high, low], axis=1)
            term = dot(both, jnp.concatenate([tile, tile], axis=0))
            if k == 0 and slot == 0:
                total[...] = term
            else:
                total[...] += term
    for j in range(4):
        out[0, j] = total[:, j * TILE : (j + 1) * TILE]
        out[1, j] = total[:, j * TILE : (j + 1) * TILE]


def spec(shape, index=None):
    if index is None:
        zeros = (0,) * len(shape)
        return pl.BlockSpec(shape, lambda *_: zeros)
    return pl.BlockSpec(shape, index)


def params():
    return pltpu.CompilerParams(vmem_limit_bytes=VMEM)


def cost(flops, moved):
    return pl.CostEstimate(flops=flops, bytes_accessed=moved, transcendentals=0)


APPLY_COST = 6 * 2 * TILE * GROUPS * WIDE * RANK


def shaped(*shape, dtype=f32):
    return jax.ShapeDtypeStruct(shape, dtype)


def group(*shape):
    return spec((1,) + shape, lambda i, *_: (i,) + (0,) * len(shape))


def first_scores(x0_t, own, far):
    half_panel = shaped(4, RANK, WIDE, dtype=bf16)
    return pl.pallas_call(
        scores_kernel,
        grid=(4,),
        in_specs=[spec((RANK, TILE))] + [group(4, RANK, TILE)] * 2,
        out_specs=[group(RANK, WIDE)] * 4 + [group(TILE, WIDE)] * 2 + [spec((TILE, RANK))],
        out_shape=[half_panel] * 4 + [shaped(4, TILE, WIDE)] * 2 + [shaped(TILE, RANK)],
        scratch_shapes=[pltpu.VMEM((2 * TILE, RANK), bf16)],
        compiler_params=params(),
        cost_estimate=cost(APPLY_COST // 2, 10 << 20),
        name="first_scores",
    )(x0_t, own, far)


def first_apply(scal, scores, panels, lev, moved):
    whole = (TILE, RANK)

    def side(i, s, far):
        return i * 2 + (1 - s[1] if far else s[1])

    levels_specs = []
    for far in (False, True):
        levels_specs += [
            spec((4, 1, 1, HALF, TILE), lambda i, s, far=far: (0, side(i, s, far), s[0], 0, 0)),
            *(
                spec((n, 1, HALF, TILE), lambda i, s, far=far: (0, side(i, s, far), 0, 0))
                for n in (1, 1, 2)
            ),
        ]
    return pl.pallas_call(
        first_kernel,
        grid_spec=pltpu.PrefetchScalarGridSpec(
            num_scalar_prefetch=1,
            grid=(4,),
            in_specs=[group(TILE, WIDE)] * 2 + [group(RANK, WIDE)] * 4 + levels_specs,
            out_specs=[group(TILE, WIDE)] * 4 + [spec(whole)],
        ),
        out_shape=[shaped(4, TILE, WIDE, dtype=bf16)] * 2
        + [shaped(4, TILE, WIDE)] * 2
        + [shaped(*whole)],
        compiler_params=params(),
        cost_estimate=cost(APPLY_COST // 2, 12 << 20),
        name="first_apply",
    )(scal, *scores, *panels, lev, *moved, lev, *moved)


def next_apply(kernel, vectors, shared, outs, name):
    whole = (TILE, RANK)
    return pl.pallas_call(
        kernel,
        grid=(4,),
        in_specs=[spec(whole)] * len(vectors) + [group(RANK, WIDE)] * 4 + [group(TILE, WIDE)] * 2,
        out_specs=[spec(whole)] * outs,
        out_shape=[shaped(*whole)] * outs,
        scratch_shapes=[pltpu.VMEM((2 * TILE, RANK), bf16)],
        compiler_params=params(),
        cost_estimate=cost(APPLY_COST, 6 << 20),
        name=name,
    )(*vectors, *shared)


def shift(value, axis, size, by):
    return lax.ppermute(value, axis, [(i, (i + by) % size) for i in range(size)])


def flip(value, axis, size, bit):
    return lax.ppermute(value, axis, [(i, i ^ bit) for i in range(size)])


def pick(value, index, axis=0):
    return lax.dynamic_index_in_dim(value, index, axis, keepdims=False)


VMEM = 16777216


def everyone(value, axis, size):
    copies = jnp.broadcast_to(value[None], (size,) + value.shape)
    return lax.all_to_all(copies, axis, split_axis=0, concat_axis=0, tiled=True)


def per_device(factors_in, items, tile_user, levels):
    y, zh, x, core, rep = (lax.axis_index(name) for name in AXES)
    half, parity = rep // 2, rep % 2
    inside = y // 2 == parity
    strip = RANK // 4
    tie = lax.optimization_barrier

    lev = levels[0].reshape(32, 2, HALF, TILE)
    other = pick(lev, 1 - half, 1)
    chunks = (other[:8], other[8:16], other[16:])
    users = factors_in.T.reshape(strip, 2, TILE)
    kept = lax.dynamic_slice_in_dim(users, half * HALF, HALF, 2).reshape(strip, TILE)
    given = lax.dynamic_slice_in_dim(users, (1 - half) * HALF, HALF, 2).reshape(strip, TILE)
    blocks = jnp.zeros((8, TILE), f32).at[0, :32].set(tile_user[0].astype(f32))
    given = jnp.concatenate([given, blocks])
    panel = items.T
    panel, kept, given, chunks = tie((panel, kept, given, chunks))

    lev_b = flip(chunks[0], "rep", 4, 2)
    panel = everyone(panel, ("zh", "rep"), 8).reshape(2, RANK, TILE)
    panel, given, lev_b, *chunks = tie((panel, given, lev_b, *chunks[1:]))
    lev_c = flip(chunks[0], "rep", 4, 2)
    got = flip(given, "rep", 4, 2)
    user_b = got[strip, :32].astype(jnp.int32)
    scal = jnp.concatenate([jnp.stack([half, core]).astype(jnp.int32), tile_user[0], user_b])
    low = jnp.where(half == 0, kept, got[:strip])
    high = jnp.where(half == 0, got[:strip], kept)
    pair = jnp.stack([low, high])

    panel = everyone(panel, "y", 4).reshape(4, 2, RANK, TILE)
    panel = lax.dynamic_slice_in_dim(panel, 2 * parity, 2, 0).reshape(1, 4, RANK, TILE)
    panel, pair, scal, lev_c, last = tie((panel, pair, scal, lev_c, chunks[1]))
    lev_d = flip(last, "rep", 4, 2)
    next_pair = flip(pair, "rep", 4, 1)
    own_panels = everyone(panel, "x", 4).reshape(4, 4, RANK, TILE)
    own_panels, next_pair, lev_d = tie((own_panels, next_pair, lev_d))
    far_panels = flip(own_panels, "core", 2, 1)
    first = jnp.where(parity == 0, pair, next_pair)
    second = jnp.where(parity == 0, next_pair, pair)
    x0_t = jnp.stack([first, second], axis=1).reshape(RANK, TILE)

    *panels, own_scores, far_scores, x0 = first_scores(x0_t, own_panels, far_panels)
    *weights, target, far_target, part = first_apply(
        scal,
        (own_scores, far_scores),
        panels,
        lev.reshape(4, GROUPS, 2, HALF, TILE),
        [v.reshape(-1, GROUPS, HALF, TILE) for v in (lev_b, lev_c, lev_d)],
    )
    shared = (*panels, *weights)
    part_b = flip(part, "rep", 4, 1)

    got = flip(far_target, "core", 2, 1)
    moved = []
    for k in (1, 2, 3):
        to = (x + k) % 4
        moved.append(shift(jnp.stack([pick(target, to), pick(got, to)]), "x", 4, k))

    resid, part = next_apply(second_kernel, (part, part_b, x0), shared, 2, "second_apply")
    part_b = flip(part, "rep", 4, 1)
    x1, resid1, direc1, part = next_apply(
        third_kernel, (part, part_b, resid, x0), shared, 4, "third_apply"
    )
    part_b = flip(part, "rep", 4, 1)
    part_b, moved = tie((part_b, moved))
    solved = pl.pallas_call(
        last_kernel,
        out_shape=shaped(TILE, RANK),
        compiler_params=params(),
        cost_estimate=cost(TILE * RANK * 10, 6 * TILE * RANK * 4),
        name="last_update",
    )(part, part_b, resid1, direc1, x1)

    pair = jnp.stack([solved, flip(solved, "core", 2, 1)])
    vectors = everyone(pair, "x", 4)

    smem = pl.BlockSpec(memory_space=pltpu.SMEM)
    vmem = pl.BlockSpec(memory_space=pltpu.VMEM)
    terms = pl.pallas_call(
        rhs_kernel,
        in_specs=[smem] + [vmem] * 6,
        out_shape=shaped(2, 4, RANK, TILE),
        scratch_shapes=[pltpu.VMEM((RANK, WIDE), f32)],
        compiler_params=params(),
        cost_estimate=cost(4 * 1024 * RANK * WIDE, 4 << 20),
        name="rhs_terms",
    )(jnp.stack([x, core]).astype(jnp.int32), vectors, target, got, *moved)

    terms, solved = tie((terms, solved))
    strips = solved.reshape(TILE, 4, strip)
    sent = flip(pick(strips, rep ^ 2, 1), "rep", 4, 2)
    kept = pick(strips, rep, 1)
    low = jnp.where(half == 0, kept, sent).reshape(2, HALF, strip)
    high = jnp.where(half == 0, sent, kept).reshape(2, HALF, strip)
    factors = jnp.stack([low, high], axis=1).reshape(2 * TILE, strip)

    summed = lax.all_to_all(
        terms.reshape(4, 8, strip, TILE), "y", split_axis=0, concat_axis=0, tiled=True
    ).sum(axis=0)
    summed, factors = tie((summed, factors))
    pieces = lax.all_to_all(
        summed, ("zh", "rep"), split_axis=0, concat_axis=0, tiled=True
    )
    chosen = pick(pieces.reshape(2, 2, 2, strip, TILE), y // 2, 2)
    scale = (2 * 64 * TILE) ** -0.5
    item_rhs = jnp.sum(chosen, axis=(0, 1)).T * (scale * STEP)
    return factors, item_rhs


def solution(mesh):
    fine = Mesh(np.asarray(mesh.devices).reshape(SIZES), AXES)
    rows = P(BLK, "rep")
    return jax.shard_map(
        per_device,
        mesh=fine,
        in_specs=(rows, rows, rows, P(BLK, "rep", None, None)),
        out_specs=(rows, rows),
        check_vma=False,
    )
```

```python
import functools

import jax
import jax.numpy as jnp
import numpy as np
from jax import lax
from jax.experimental import pallas as pl
from jax.experimental.pallas import tpu as pltpu
from jax.sharding import Mesh, PartitionSpec as P

ITERS = 2
AXES = ("y", "zh", "x", "core", "rep")
SIZES = (4, 2, 4, 2, 4)
BLK = ("y", "zh", "x", "core")
RANK = 256
TILE = 128
HALF = TILE // 2
GROUPS = 8
WIDE = 4 * TILE
RIDGE = 0.1
STEP = 0.1
f32 = jnp.float32
bf16 = jnp.bfloat16


def split(value):
    high = value.astype(bf16)
    low = (value - high.astype(f32)).astype(bf16)
    return high, low


def dot(a, b):
    return lax.dot_general(a, b, (((1,), (0,)), ((), ())), preferred_element_type=f32)


def dot_t(a, b):
    return lax.dot_general(a, b, (((1,), (1,)), ((), ())), preferred_element_type=f32)


def scores_of(stacked, panel_hi, panel_lo):
    both = dot(stacked, panel_hi)
    return both[:TILE] + both[TILE:] + dot(stacked[:TILE], panel_lo)


def project(mixed, panel_hi, panel_lo):
    high, low = split(mixed)
    both = dot_t(jnp.concatenate([high, low], axis=0), panel_hi)
    return both[:TILE] + both[TILE:] + dot_t(high, panel_lo)


def store_split(vectors, stacked):
    high, low = split(vectors)
    stacked[:TILE] = high
    stacked[TILE:] = low


def scores_kernel(
    x0_t, own, far, own_hi, own_lo, far_hi, far_lo, own_scores, far_scores, x0, stacked
):
    @pl.when(pl.program_id(0) == 0)
    def _():
        start = x0_t[...].T
        x0[...] = start
        store_split(start, stacked)

    sides = ((own, own_hi, own_lo, own_scores), (far, far_hi, far_lo, far_scores))
    for panels, hi, lo, scores in sides:
        for j in range(4):
            cols = slice(j * TILE, (j + 1) * TILE)
            high, low = split(panels[0, j])
            hi[0, :, cols] = high
            lo[0, :, cols] = low
        scores[0] = scores_of(stacked[...], hi[0], lo[0])


def first_kernel(scal, *refs):
    own_scores, far_scores, own_hi, own_lo, far_hi, far_lo, *refs = refs
    *refs, own_weight, far_weight, own_target, far_target, part = refs
    count = len(refs) // 2
    own_a, own_moved = refs[0], refs[1:count]
    far_a, far_moved = refs[count], refs[count + 1 :]
    i = pl.program_id(0)
    x, core = scal[2], scal[1]
    at = (lax.rem(x + 4 - i, 4) if REL else i) * 2

    @pl.when(i == 0)
    def _():
        part[...] = jnp.zeros_like(part)

    sides = (
        (core, own_scores, own_hi, own_lo, own_a, own_moved, own_weight, own_target),
        (1 - core, far_scores, far_hi, far_lo, far_a, far_moved, far_weight, far_target),
    )
    for which, scores, hi, lo, lev_a, moved, weight, target in sides:
        for j in range(4):
            cols = slice(j * TILE, (j + 1) * TILE)
            tile = j * GROUPS + at + which
            a1 = scal[3 + tile].astype(f32)
            b1 = scal[35 + tile].astype(f32)
            a0, b0 = 1.0 - a1, 1.0 - b1
            la = lev_a[j, 0, 0].astype(f32)
            lb = jnp.concatenate([rows[j, 0] for rows in moved], axis=0).astype(f32)
            ta = la + jnp.where(la > 0, 10.0, 0.0)
            tb = lb + jnp.where(lb > 0, 10.0, 0.0)
            weight[0, :HALF, cols] = (10.0 + a0 * la + b0 * lb).astype(bf16)
            weight[0, HALF:, cols] = (10.0 + a1 * la + b1 * lb).astype(bf16)
            target[0, :HALF, cols] = a0 * ta + b0 * tb
            target[0, HALF:, cols] = a1 * ta + b1 * tb
        mixed = STEP * (target[0] - weight[0].astype(f32) * scores[0])
        part[...] += project(mixed, hi[0], lo[0])


def apply_step(shared, part, stacked):
    own_hi, own_lo, far_hi, far_lo, own_weight, far_weight = shared
    for hi, lo, weight in ((own_hi, own_lo, own_weight), (far_hi, far_lo, far_weight)):
        scores = scores_of(stacked[...], hi[0], lo[0])
        mixed = STEP * (weight[0].astype(f32) * scores)
        part[...] += project(mixed, hi[0], lo[0])


def second_kernel(pa, pb, x0, *refs):
    shared, (resid, part, stacked) = refs[:6], refs[6:]

    @pl.when(pl.program_id(0) == 0)
    def _():
        start = pa[...] + pb[...] - RIDGE * x0[...]
        resid[...] = start
        store_split(start, stacked)
        part[...] = jnp.zeros_like(part)

    apply_step(shared, part, stacked)


def third_kernel(pa, pb, resid, x0, *refs):
    shared, (x1, resid1, direc1, part, stacked) = refs[:6], refs[6:]

    @pl.when(pl.program_id(0) == 0)
    def _():
        direc = resid[...]
        image = pa[...] + pb[...] + RIDGE * direc
        rho = jnp.sum(direc * direc, axis=1, keepdims=True)
        alpha = rho / jnp.sum(direc * image, axis=1, keepdims=True)
        x1[...] = x0[...] + alpha * direc
        after = direc - alpha * image
        resid1[...] = after
        rho_next = jnp.sum(after * after, axis=1, keepdims=True)
        ahead = after + (rho_next / rho) * direc
        direc1[...] = ahead
        store_split(ahead, stacked)
        part[...] = jnp.zeros_like(part)

    apply_step(shared, part, stacked)


def last_kernel(pa, pb, resid, direc, x1, out, copies):
    image = pa[...] + pb[...] + RIDGE * direc[...]
    rho = jnp.sum(resid[...] * resid[...], axis=1, keepdims=True)
    alpha = rho / jnp.sum(direc[...] * image, axis=1, keepdims=True)
    solved = x1[...] + alpha * direc[...]
    out[...] = solved
    for k in range(4):
        copies[k] = solved


def rhs_kernel(scal, own_vectors, far_vectors, own, got, t1, t2, t3, out, total):
    x = scal[0]
    for k in range(4):
        source = lax.rem(x + k, 4) if FG == "a2a" else k
        for slot in range(2):
            chunk = (own_vectors, far_vectors)[slot][source]
            if k == 0:
                tile = (own, got)[slot][0 if REL else x]
            else:
                tile = (t1, t2, t3)[k - 1][slot]
            tile = tile.astype(bf16)
            high, low = split(chunk.T)
            both = jnp.concatenate([high, low], axis=1)
            term = dot(both, jnp.concatenate([tile, tile], axis=0))
            if k == 0 and slot == 0:
                total[...] = term
            else:
                total[...] += term
    for j in range(4):
        out[0, j] = total[:, j * TILE : (j + 1) * TILE]
        out[1, j] = total[:, j * TILE : (j + 1) * TILE]


def spec(shape, index=None):
    if index is None:
        zeros = (0,) * len(shape)
        return pl.BlockSpec(shape, lambda *_: zeros)
    return pl.BlockSpec(shape, index)


def params():
    return pltpu.CompilerParams(vmem_limit_bytes=VMEM)


def cost(flops, moved):
    return pl.CostEstimate(flops=flops, bytes_accessed=moved, transcendentals=0)


APPLY_COST = 6 * 2 * TILE * GROUPS * WIDE * RANK


def shaped(*shape, dtype=f32):
    return jax.ShapeDtypeStruct(shape, dtype)


def group(*shape):
    return spec((1,) + shape, lambda i, *_: (i,) + (0,) * len(shape))


def first_scores(x0_t, own, far):
    half_panel = shaped(4, RANK, WIDE, dtype=bf16)
    return pl.pallas_call(
        scores_kernel,
        grid=(4,),
        in_specs=[spec((RANK, TILE))] + [group(4, RANK, TILE)] * 2,
        out_specs=[group(RANK, WIDE)] * 4 + [group(TILE, WIDE)] * 2 + [spec((TILE, RANK))],
        out_shape=[half_panel] * 4 + [shaped(4, TILE, WIDE)] * 2 + [shaped(TILE, RANK)],
        scratch_shapes=[pltpu.VMEM((2 * TILE, RANK), bf16)],
        compiler_params=params(),
        cost_estimate=cost(APPLY_COST // 2, 10 << 20),
        name="first_scores",
    )(x0_t, own, far)


def first_apply(scal, scores, panels, lev, moved):
    whole = (TILE, RANK)

    def side(i, s, far):
        return (lax.rem(s[2] + 4 - i, 4) if REL else i) * 2 + (1 - s[1] if far else s[1])

    levels_specs = []
    for far in (False, True):
        levels_specs += [
            spec((4, 1, 1, HALF, TILE), lambda i, s, far=far: (0, side(i, s, far), s[0], 0, 0)),
            *(
                spec((4, 1, n, TILE), lambda i, s, far=far: (0, side(i, s, far), 0, 0))
                for n in CHUNKS
            ),
        ]
    return pl.pallas_call(
        first_kernel,
        grid_spec=pltpu.PrefetchScalarGridSpec(
            num_scalar_prefetch=1,
            grid=(4,),
            in_specs=[group(TILE, WIDE)] * 2 + [group(RANK, WIDE)] * 4 + levels_specs,
            out_specs=[group(TILE, WIDE)] * 4 + [spec(whole)],
        ),
        out_shape=[shaped(4, TILE, WIDE, dtype=bf16)] * 2
        + [shaped(4, TILE, WIDE)] * 2
        + [shaped(*whole)],
        compiler_params=params(),
        cost_estimate=cost(APPLY_COST // 2, 12 << 20),
        name="first_apply",
    )(scal, *scores, *panels, lev, *moved, lev, *moved)


def next_apply(kernel, vectors, shared, outs, name):
    whole = (TILE, RANK)
    return pl.pallas_call(
        kernel,
        grid=(4,),
        in_specs=[spec(whole)] * len(vectors) + [group(RANK, WIDE)] * 4 + [group(TILE, WIDE)] * 2,
        out_specs=[spec(whole)] * outs,
        out_shape=[shaped(*whole)] * outs,
        scratch_shapes=[pltpu.VMEM((2 * TILE, RANK), bf16)],
        compiler_params=params(),
        cost_estimate=cost(APPLY_COST, 6 << 20),
        name=name,
    )(*vectors, *shared)


def shift(value, axis, size, by):
    return lax.ppermute(value, axis, [(i, (i + by) % size) for i in range(size)])


def flip(value, axis, size, bit):
    return lax.ppermute(value, axis, [(i, i ^ bit) for i in range(size)])


def pick(value, index, axis=0):
    return lax.dynamic_index_in_dim(value, index, axis, keepdims=False)


VMEM = 16777216
FG = 'a2a'
XS = 'perm'
REL = 1
YS = 'a2a'
X0 = 'z'
CHUNKS = (8,16,32,8)


def everyone(value, axis, size):
    copies = jnp.broadcast_to(value[None], (size,) + value.shape)
    return lax.all_to_all(copies, axis, split_axis=0, concat_axis=0, tiled=True)


def along_y(value, move):
    pairs = [
        (s * 4 + r, move(s) * 4 + r) for s in range(4) for r in range(4) if s // 2 == r % 2
    ]
    return lax.ppermute(value, ("y", "rep"), pairs)


def per_device(factors_in, items, tile_user, levels):
    y, zh, x, core, rep = (lax.axis_index(name) for name in AXES)
    half, parity = rep // 2, rep % 2
    inside = y // 2 == parity
    strip = RANK // 4
    tie = lax.optimization_barrier

    lev = levels[0].reshape(32, 2, HALF, TILE)
    other = pick(lev, 1 - half, 1)
    parts, at = [], 0
    for rows in CHUNKS:
        parts.append(other[:, at : at + rows])
        at += rows
    users = factors_in.T.reshape(strip, 2, TILE)
    kept = lax.dynamic_slice_in_dim(users, half * HALF, HALF, 2).reshape(strip, TILE)
    given = lax.dynamic_slice_in_dim(users, (1 - half) * HALF, HALF, 2).reshape(strip, TILE)
    blocks = jnp.zeros((8, TILE), f32).at[0, :32].set(tile_user[0].astype(f32))
    given = jnp.concatenate([given, blocks])

    moved_levels = [flip(parts[0], "rep", 4, 2)]
    if X0 == "z":
        got = flip(given, "rep", 4, 2)
    panel = everyone(items.T, ("zh", "rep"), 8).reshape(2, RANK, TILE)
    if X0 == "y":
        panel, given, moved_levels, *parts = tie((panel, given, moved_levels, *parts[1:]))
        got = flip(given, "rep", 4, 2)
    else:
        panel, got, moved_levels, *parts = tie((panel, got, moved_levels, *parts[1:]))

    moved_levels.append(flip(parts[0], "rep", 4, 2))
    low = jnp.where(half == 0, kept, got[:strip])
    high = jnp.where(half == 0, got[:strip], kept)
    pair = jnp.stack([low, high])
    if X0 == "z":
        next_pair = flip(pair, "rep", 4, 1)
    if YS == "perm":
        inside = y // 2 == parity
        beside = along_y(panel, lambda s: s ^ 1)
        across = along_y(panel, lambda s: 3 - s)
        beyond = along_y(panel, lambda s: (s + 2) % 4)
        same = jnp.where(inside, panel, beyond)
        odd = jnp.where(inside, beside, across)
        even = y % 2 == 0
        panel = jnp.stack([jnp.where(even, same, odd), jnp.where(even, odd, same)])
    elif YS == "two":
        inside = y // 2 == parity
        across = along_y(panel, lambda s: 3 - s)
        now = jnp.where(inside, panel, across)
        beside = flip(now, "y", 4, 1)
        even = (y % 2 == 0) == inside
        panel = jnp.stack([jnp.where(even, now, beside), jnp.where(even, beside, now)])
    else:
        panel = everyone(panel, "y", 4).reshape(4, 2, RANK, TILE)
        panel = lax.dynamic_slice_in_dim(panel, 2 * parity, 2, 0)
    panel = panel.reshape(4, RANK, TILE)
    if X0 == "y":
        panel, pair, got, moved_levels, *parts = tie((panel, pair, got, moved_levels, *parts[1:]))
        next_pair = flip(pair, "rep", 4, 1)
    else:
        panel, pair, next_pair, got, moved_levels, *parts = tie(
            (panel, pair, next_pair, got, moved_levels, *parts[1:])
        )

    moved_levels.append(flip(parts[0], "rep", 4, 2))
    if XS == "perm":
        own_panels = jnp.stack([panel] + [shift(panel, "x", 4, k) for k in (1, 2, 3)])
    else:
        own_panels = everyone(panel, "x", 4).reshape(4, 4, RANK, TILE)
    own_panels, pair, next_pair, got, moved_levels, *parts = tie(
        (own_panels, pair, next_pair, got, moved_levels, *parts[1:])
    )
    moved_levels = moved_levels + [flip(rows, "rep", 4, 2) for rows in parts]
    far_panels = flip(own_panels, "core", 2, 1)
    user_b = got[strip, :32].astype(jnp.int32)
    place = jnp.stack([half, core, x]).astype(jnp.int32)
    scal = jnp.concatenate([place, tile_user[0], user_b])
    first = jnp.where(parity == 0, pair, next_pair)
    second = jnp.where(parity == 0, next_pair, pair)
    x0_t = jnp.stack([first, second], axis=1).reshape(RANK, TILE)

    *panels, own_scores, far_scores, x0 = first_scores(x0_t, own_panels, far_panels)
    *weights, target, far_target, part = first_apply(
        scal,
        (own_scores, far_scores),
        panels,
        lev.reshape(4, GROUPS, 2, HALF, TILE),
        [rows.reshape(4, GROUPS, -1, TILE) for rows in moved_levels],
    )
    shared = (*panels, *weights)
    part_b = flip(part, "rep", 4, 1)

    got = flip(far_target, "core", 2, 1)
    moved = []
    for k in (1, 2, 3):
        to = k if REL else (x - k) % 4
        moved.append(shift(jnp.stack([pick(target, to), pick(got, to)]), "x", 4, -k))

    resid, part = next_apply(second_kernel, (part, part_b, x0), shared, 2, "second_apply")
    part_b = flip(part, "rep", 4, 1)
    x1, resid1, direc1, part = next_apply(
        third_kernel, (part, part_b, resid, x0), shared, 4, "third_apply"
    )
    part_b = flip(part, "rep", 4, 1)
    part_b, moved = tie((part_b, moved))
    solved, copies = pl.pallas_call(
        last_kernel,
        out_shape=[shaped(TILE, RANK), shaped(4, TILE, RANK)],
        compiler_params=params(),
        cost_estimate=cost(TILE * RANK * 10, 10 * TILE * RANK * 4),
        name="last_update",
    )(part, part_b, resid1, direc1, x1)

    if FG == "a2a":
        vectors = lax.all_to_all(copies, "x", split_axis=0, concat_axis=0, tiled=True)
    else:
        vectors = jnp.stack([solved] + [shift(solved, "x", 4, -k) for k in (1, 2, 3)])
    far_vectors = flip(vectors, "core", 2, 1)

    smem = pl.BlockSpec(memory_space=pltpu.SMEM)
    vmem = pl.BlockSpec(memory_space=pltpu.VMEM)
    terms = pl.pallas_call(
        rhs_kernel,
        in_specs=[smem] + [vmem] * 7,
        out_shape=shaped(2, 4, RANK, TILE),
        scratch_shapes=[pltpu.VMEM((RANK, WIDE), f32)],
        compiler_params=params(),
        cost_estimate=cost(4 * 1024 * RANK * WIDE, 4 << 20),
        name="rhs_terms",
    )(jnp.stack([x, core]).astype(jnp.int32), vectors, far_vectors, target, got, *moved)

    terms, solved = tie((terms, solved))
    strips = solved.reshape(TILE, 4, strip)
    sent = flip(pick(strips, rep ^ 2, 1), "rep", 4, 2)
    kept = pick(strips, rep, 1)
    low = jnp.where(half == 0, kept, sent).reshape(2, HALF, strip)
    high = jnp.where(half == 0, sent, kept).reshape(2, HALF, strip)
    factors = jnp.stack([low, high], axis=1).reshape(2 * TILE, strip)

    summed = lax.all_to_all(
        terms.reshape(4, 8, strip, TILE), "y", split_axis=0, concat_axis=0, tiled=True
    ).sum(axis=0)
    summed, factors = tie((summed, factors))
    pieces = lax.all_to_all(
        summed, ("zh", "rep"), split_axis=0, concat_axis=0, tiled=True
    )
    chosen = pick(pieces.reshape(2, 2, 2, strip, TILE), y // 2, 2)
    scale = (2 * 64 * TILE) ** -0.5
    item_rhs = jnp.sum(chosen, axis=(0, 1)).T * (scale * STEP)
    return factors, item_rhs


def solution(mesh):
    fine = Mesh(np.asarray(mesh.devices).reshape(SIZES), AXES)
    rows = P(BLK, "rep")
    return jax.shard_map(
        per_device,
        mesh=fine,
        in_specs=(rows, rows, rows, P(BLK, "rep", None, None)),
        out_specs=(rows, rows),
        check_vma=False,
    )
```

```python
import functools

import jax
import jax.numpy as jnp
import numpy as np
from jax import lax
from jax.experimental import pallas as pl
from jax.experimental.pallas import tpu as pltpu
from jax.sharding import Mesh, PartitionSpec as P

ITERS = 2
AXES = ("y", "zh", "x", "core", "rep")
SIZES = (4, 2, 4, 2, 4)
BLK = ("y", "zh", "x", "core")
RANK = 256
TILE = 128
HALF = TILE // 2
GROUPS = 8
WIDE = 4 * TILE
RIDGE = 0.1
STEP = 0.1
f32 = jnp.float32
bf16 = jnp.bfloat16


def split(value):
    high = value.astype(bf16)
    low = (value - high.astype(f32)).astype(bf16)
    return high, low


def dot(a, b):
    return lax.dot_general(a, b, (((1,), (0,)), ((), ())), preferred_element_type=f32)


def dot_t(a, b):
    return lax.dot_general(a, b, (((1,), (1,)), ((), ())), preferred_element_type=f32)


def scores_of(stacked, panel_hi, panel_lo):
    both = dot(stacked, panel_hi)
    return both[:TILE] + both[TILE:] + dot(stacked[:TILE], panel_lo)


def project(mixed, panel_hi, panel_lo):
    high, low = split(mixed)
    both = dot_t(jnp.concatenate([high, low], axis=0), panel_hi)
    return both[:TILE] + both[TILE:] + dot_t(high, panel_lo)


def store_split(vectors, stacked):
    high, low = split(vectors)
    stacked[:TILE] = high
    stacked[TILE:] = low


def scores_kernel(
    x0_t, own, far, own_hi, own_lo, far_hi, far_lo, own_scores, far_scores, x0, stacked
):
    @pl.when(pl.program_id(0) == 0)
    def _():
        start = x0_t[...].T
        x0[...] = start
        store_split(start, stacked)

    sides = ((own, own_hi, own_lo, own_scores), (far, far_hi, far_lo, far_scores))
    for panels, hi, lo, scores in sides:
        for j in range(4):
            cols = slice(j * TILE, (j + 1) * TILE)
            high, low = split(panels[0, j])
            hi[0, :, cols] = high
            lo[0, :, cols] = low
        scores[0] = scores_of(stacked[...], hi[0], lo[0])


def first_kernel(scal, *refs):
    own_scores, far_scores, own_hi, own_lo, far_hi, far_lo, *refs = refs
    *refs, own_weight, far_weight, own_target, far_target, part = refs
    count = len(refs) // 2
    own_a, own_moved = refs[0], refs[1:count]
    far_a, far_moved = refs[count], refs[count + 1 :]
    i = pl.program_id(0)
    x, core = scal[2], scal[1]
    at = (lax.rem(x + 4 - i, 4) if REL else i) * 2

    @pl.when(i == 0)
    def _():
        part[...] = jnp.zeros_like(part)

    sides = (
        (core, own_scores, own_hi, own_lo, own_a, own_moved, own_weight, own_target),
        (1 - core, far_scores, far_hi, far_lo, far_a, far_moved, far_weight, far_target),
    )
    for which, scores, hi, lo, lev_a, moved, weight, target in sides:
        for j in range(4):
            cols = slice(j * TILE, (j + 1) * TILE)
            tile = j * GROUPS + at + which
            a1 = scal[3 + tile].astype(f32)
            b1 = scal[35 + tile].astype(f32)
            a0, b0 = 1.0 - a1, 1.0 - b1
            la = lev_a[j, 0, 0].astype(f32)
            lb = jnp.concatenate([rows[j, 0] for rows in moved], axis=0).astype(f32)
            ta = la + jnp.where(la > 0, 10.0, 0.0)
            tb = lb + jnp.where(lb > 0, 10.0, 0.0)
            weight[0, :HALF, cols] = (10.0 + a0 * la + b0 * lb).astype(bf16)
            weight[0, HALF:, cols] = (10.0 + a1 * la + b1 * lb).astype(bf16)
            target[0, :HALF, cols] = a0 * ta + b0 * tb
            target[0, HALF:, cols] = a1 * ta + b1 * tb
        mixed = STEP * (target[0] - weight[0].astype(f32) * scores[0])
        part[...] += project(mixed, hi[0], lo[0])


def apply_step(shared, part, stacked):
    own_hi, own_lo, far_hi, far_lo, own_weight, far_weight = shared
    for hi, lo, weight in ((own_hi, own_lo, own_weight), (far_hi, far_lo, far_weight)):
        scores = scores_of(stacked[...], hi[0], lo[0])
        mixed = STEP * (weight[0].astype(f32) * scores)
        part[...] += project(mixed, hi[0], lo[0])


def second_kernel(pa, pb, x0, *refs):
    shared, (resid, part, stacked) = refs[:6], refs[6:]

    @pl.when(pl.program_id(0) == 0)
    def _():
        start = pa[...] + pb[...] - RIDGE * x0[...]
        resid[...] = start
        store_split(start, stacked)
        part[...] = jnp.zeros_like(part)

    apply_step(shared, part, stacked)


def third_kernel(pa, pb, resid, x0, *refs):
    shared, (x1, resid1, direc1, part, stacked) = refs[:6], refs[6:]

    @pl.when(pl.program_id(0) == 0)
    def _():
        direc = resid[...]
        image = pa[...] + pb[...] + RIDGE * direc
        rho = jnp.sum(direc * direc, axis=1, keepdims=True)
        alpha = rho / jnp.sum(direc * image, axis=1, keepdims=True)
        x1[...] = x0[...] + alpha * direc
        after = direc - alpha * image
        resid1[...] = after
        rho_next = jnp.sum(after * after, axis=1, keepdims=True)
        ahead = after + (rho_next / rho) * direc
        direc1[...] = ahead
        store_split(ahead, stacked)
        part[...] = jnp.zeros_like(part)

    apply_step(shared, part, stacked)


def last_kernel(pa, pb, resid, direc, x1, out, copies):
    image = pa[...] + pb[...] + RIDGE * direc[...]
    rho = jnp.sum(resid[...] * resid[...], axis=1, keepdims=True)
    alpha = rho / jnp.sum(direc[...] * image, axis=1, keepdims=True)
    solved = x1[...] + alpha * direc[...]
    out[...] = solved
    for k in range(4):
        copies[k] = solved


def rhs_kernel(scal, own_vectors, far_vectors, own, got, t1, t2, t3, out, total):
    x = scal[0]
    for k in range(4):
        source = lax.rem(x + k, 4) if FG == "a2a" else k
        for slot in range(2):
            chunk = (own_vectors, far_vectors)[slot][source]
            if k == 0:
                tile = (own, got)[slot][0 if REL else x]
            else:
                tile = (t1, t2, t3)[k - 1][slot]
            tile = tile.astype(bf16)
            high, low = split(chunk.T)
            both = jnp.concatenate([high, low], axis=1)
            term = dot(both, jnp.concatenate([tile, tile], axis=0))
            if k == 0 and slot == 0:
                total[...] = term
            else:
                total[...] += term
    for j in range(4):
        out[0, j] = total[:, j * TILE : (j + 1) * TILE]
        out[1, j] = total[:, j * TILE : (j + 1) * TILE]


def spec(shape, index=None):
    if index is None:
        zeros = (0,) * len(shape)
        return pl.BlockSpec(shape, lambda *_: zeros)
    return pl.BlockSpec(shape, index)


def params():
    return pltpu.CompilerParams(vmem_limit_bytes=VMEM)


def cost(flops, moved):
    return pl.CostEstimate(flops=flops, bytes_accessed=moved, transcendentals=0)


APPLY_COST = 6 * 2 * TILE * GROUPS * WIDE * RANK


def shaped(*shape, dtype=f32):
    return jax.ShapeDtypeStruct(shape, dtype)


def group(*shape):
    return spec((1,) + shape, lambda i, *_: (i,) + (0,) * len(shape))


def first_scores(x0_t, own, far):
    half_panel = shaped(4, RANK, WIDE, dtype=bf16)
    return pl.pallas_call(
        scores_kernel,
        grid=(4,),
        in_specs=[spec((RANK, TILE))] + [group(4, RANK, TILE)] * 2,
        out_specs=[group(RANK, WIDE)] * 4 + [group(TILE, WIDE)] * 2 + [spec((TILE, RANK))],
        out_shape=[half_panel] * 4 + [shaped(4, TILE, WIDE)] * 2 + [shaped(TILE, RANK)],
        scratch_shapes=[pltpu.VMEM((2 * TILE, RANK), bf16)],
        compiler_params=params(),
        cost_estimate=cost(APPLY_COST // 2, 10 << 20),
        name="first_scores",
    )(x0_t, own, far)


def first_apply(scal, scores, panels, lev, moved):
    whole = (TILE, RANK)

    def side(i, s, far):
        return (lax.rem(s[2] + 4 - i, 4) if REL else i) * 2 + (1 - s[1] if far else s[1])

    levels_specs = []
    for far in (False, True):
        levels_specs += [
            spec((4, 1, 1, HALF, TILE), lambda i, s, far=far: (0, side(i, s, far), s[0], 0, 0)),
            *(
                spec((4, 1, n, TILE), lambda i, s, far=far: (0, side(i, s, far), 0, 0))
                for n in CHUNKS
            ),
        ]
    return pl.pallas_call(
        first_kernel,
        grid_spec=pltpu.PrefetchScalarGridSpec(
            num_scalar_prefetch=1,
            grid=(4,),
            in_specs=[group(TILE, WIDE)] * 2 + [group(RANK, WIDE)] * 4 + levels_specs,
            out_specs=[group(TILE, WIDE)] * 4 + [spec(whole)],
        ),
        out_shape=[shaped(4, TILE, WIDE, dtype=bf16)] * 2
        + [shaped(4, TILE, WIDE)] * 2
        + [shaped(*whole)],
        compiler_params=params(),
        cost_estimate=cost(APPLY_COST // 2, 12 << 20),
        name="first_apply",
    )(scal, *scores, *panels, lev, *moved, lev, *moved)


def next_apply(kernel, vectors, shared, outs, name):
    whole = (TILE, RANK)
    return pl.pallas_call(
        kernel,
        grid=(4,),
        in_specs=[spec(whole)] * len(vectors) + [group(RANK, WIDE)] * 4 + [group(TILE, WIDE)] * 2,
        out_specs=[spec(whole)] * outs,
        out_shape=[shaped(*whole)] * outs,
        scratch_shapes=[pltpu.VMEM((2 * TILE, RANK), bf16)],
        compiler_params=params(),
        cost_estimate=cost(APPLY_COST, 6 << 20),
        name=name,
    )(*vectors, *shared)


def shift(value, axis, size, by):
    return lax.ppermute(value, axis, [(i, (i + by) % size) for i in range(size)])


def flip(value, axis, size, bit):
    return lax.ppermute(value, axis, [(i, i ^ bit) for i in range(size)])


def pick(value, index, axis=0):
    return lax.dynamic_index_in_dim(value, index, axis, keepdims=False)


VMEM = 16777216
FG = 'a2a'
XS = 'perm'
YS = 'a2a'
REL = 1
FP = 'early'
TAIL = 'a2a'
XC = 0
NP = 'y'
CHUNKS = (56,8)


def everyone(value, axis, size):
    copies = jnp.broadcast_to(value[None], (size,) + value.shape)
    return lax.all_to_all(copies, axis, split_axis=0, concat_axis=0, tiled=True)


def along_y(value, move):
    pairs = [
        (s * 4 + r, move(s) * 4 + r) for s in range(4) for r in range(4) if s // 2 == r % 2
    ]
    return lax.ppermute(value, ("y", "rep"), pairs)


def per_device(factors_in, items, tile_user, levels):
    y, zh, x, core, rep = (lax.axis_index(name) for name in AXES)
    half, parity = rep // 2, rep % 2
    inside = y // 2 == parity
    strip = RANK // 4
    tie = lax.optimization_barrier

    lev = levels[0].reshape(32, 2, HALF, TILE)
    other = pick(lev, 1 - half, 1)
    parts, at = [], 0
    for rows in CHUNKS:
        parts.append(other[:, at : at + rows])
        at += rows
    users = factors_in.T.reshape(strip, 2, TILE)
    kept = lax.dynamic_slice_in_dim(users, half * HALF, HALF, 2).reshape(strip, TILE)
    given = lax.dynamic_slice_in_dim(users, (1 - half) * HALF, HALF, 2).reshape(strip, TILE)
    blocks = jnp.zeros((8, TILE), f32).at[0, :32].set(tile_user[0].astype(f32))
    given = jnp.concatenate([given, blocks])

    moved_levels = []
    got = flip(given, "rep", 4, 2)
    low = jnp.where(half == 0, kept, got[:strip])
    high = jnp.where(half == 0, got[:strip], kept)
    pair = jnp.stack([low, high])
    next_pair = flip(pair, "rep", 4, 1)
    panel = everyone(items.T, ("zh", "rep"), 8).reshape(2, RANK, TILE)
    if NP == "z":
        panel, pair, next_pair, got, *parts = tie((panel, pair, next_pair, got, *parts))
    else:
        panel, pair, got, *parts = tie((panel, pair, got, *parts))
        next_pair = flip(pair, "rep", 4, 1)

    moved_levels.append(flip(parts[0], "rep", 4, 2))
    if YS == "perm":
        inside = y // 2 == parity
        beside = along_y(panel, lambda s: s ^ 1)
        across = along_y(panel, lambda s: 3 - s)
        beyond = along_y(panel, lambda s: (s + 2) % 4)
        same = jnp.where(inside, panel, beyond)
        odd = jnp.where(inside, beside, across)
        even = y % 2 == 0
        panel = jnp.stack([jnp.where(even, same, odd), jnp.where(even, odd, same)])
    elif YS == "two":
        inside = y // 2 == parity
        across = along_y(panel, lambda s: 3 - s)
        now = jnp.where(inside, panel, across)
        beside = flip(now, "y", 4, 1)
        even = (y % 2 == 0) == inside
        panel = jnp.stack([jnp.where(even, now, beside), jnp.where(even, beside, now)])
    else:
        panel = everyone(panel, "y", 4).reshape(4, 2, RANK, TILE)
        panel = lax.dynamic_slice_in_dim(panel, 2 * parity, 2, 0)
    panel = panel.reshape(4, RANK, TILE)
    panel, pair, got, *parts = tie((panel, pair, got, *parts[1:]))

    if XC:
        moved_levels.append(flip(parts[0], "rep", 4, 2))
        parts = parts[1:]
    if XS == "ring":
        left, right = shift(panel, "x", 4, 1), shift(panel, "x", 4, -1)
        over = jnp.concatenate([shift(left[:2], "x", 4, 1), shift(right[2:], "x", 4, -1)])
        own_panels = jnp.stack([panel, left, over, right])
    elif XS == "perm":
        own_panels = jnp.stack([panel] + [shift(panel, "x", 4, k) for k in (1, 2, 3)])
    else:
        own_panels = everyone(panel, "x", 4).reshape(4, 4, RANK, TILE)
    own_panels, pair, next_pair, got, moved_levels, *parts = tie(
        (own_panels, pair, next_pair, got, moved_levels, *parts)
    )
    moved_levels = moved_levels + [flip(rows, "rep", 4, 2) for rows in parts]
    far_panels = flip(own_panels, "core", 2, 1)
    user_b = got[strip, :32].astype(jnp.int32)
    place = jnp.stack([half, core, x]).astype(jnp.int32)
    scal = jnp.concatenate([place, tile_user[0], user_b])
    first = jnp.where(parity == 0, pair, next_pair)
    second = jnp.where(parity == 0, next_pair, pair)
    x0_t = jnp.stack([first, second], axis=1).reshape(RANK, TILE)

    *panels, own_scores, far_scores, x0 = first_scores(x0_t, own_panels, far_panels)
    *weights, target, far_target, part = first_apply(
        scal,
        (own_scores, far_scores),
        panels,
        lev.reshape(4, GROUPS, 2, HALF, TILE),
        [rows.reshape(4, GROUPS, -1, TILE) for rows in moved_levels],
    )
    shared = (*panels, *weights)
    part_b = flip(part, "rep", 4, 1)

    got = flip(far_target, "core", 2, 1)
    moved = []
    for k in (1, 2, 3):
        to = k if REL else (x - k) % 4
        moved.append(shift(jnp.stack([pick(target, to), pick(got, to)]), "x", 4, -k))

    resid, part = next_apply(second_kernel, (part, part_b, x0), shared, 2, "second_apply")
    part_b = flip(part, "rep", 4, 1)
    x1, resid1, direc1, part = next_apply(
        third_kernel, (part, part_b, resid, x0), shared, 4, "third_apply"
    )
    part_b = flip(part, "rep", 4, 1)
    part_b, moved = tie((part_b, moved))
    solved, copies = pl.pallas_call(
        last_kernel,
        out_shape=[shaped(TILE, RANK), shaped(4, TILE, RANK)],
        compiler_params=params(),
        cost_estimate=cost(TILE * RANK * 10, 10 * TILE * RANK * 4),
        name="last_update",
    )(part, part_b, resid1, direc1, x1)

    if FG == "a2a":
        vectors = lax.all_to_all(copies, "x", split_axis=0, concat_axis=0, tiled=True)
    elif FG == "ring":
        left, right = shift(solved, "x", 4, -1), shift(solved, "x", 4, 1)
        over = jnp.concatenate([shift(left[:HALF], "x", 4, -1), shift(right[HALF:], "x", 4, 1)])
        vectors = jnp.stack([solved, left, over, right])
    else:
        vectors = jnp.stack([solved] + [shift(solved, "x", 4, -k) for k in (1, 2, 3)])
    far_vectors = flip(vectors, "core", 2, 1)

    smem = pl.BlockSpec(memory_space=pltpu.SMEM)
    vmem = pl.BlockSpec(memory_space=pltpu.VMEM)
    terms = pl.pallas_call(
        rhs_kernel,
        in_specs=[smem] + [vmem] * 7,
        out_shape=shaped(2, 4, RANK, TILE),
        scratch_shapes=[pltpu.VMEM((RANK, WIDE), f32)],
        compiler_params=params(),
        cost_estimate=cost(4 * 1024 * RANK * WIDE, 4 << 20),
        name="rhs_terms",
    )(jnp.stack([x, core]).astype(jnp.int32), vectors, far_vectors, target, got, *moved)

    if FP == 'late':
        terms, solved = tie((terms, solved))
    strips = solved.reshape(TILE, 4, strip)
    sent = flip(pick(strips, rep ^ 2, 1), "rep", 4, 2)
    kept = pick(strips, rep, 1)
    low = jnp.where(half == 0, kept, sent).reshape(2, HALF, strip)
    high = jnp.where(half == 0, sent, kept).reshape(2, HALF, strip)
    factors = jnp.stack([low, high], axis=1).reshape(2 * TILE, strip)

    if TAIL == "one":
        pieces = lax.all_to_all(
            terms.reshape(32, strip, TILE),
            ("y", "zh", "rep"),
            split_axis=0,
            concat_axis=0,
            tiled=True,
        )
        pieces = pieces.reshape(4, 8, strip, TILE).sum(axis=0)
    else:
        if TAIL == "two":
            pair = terms.reshape(4, 8, strip, TILE)
            inside = y // 2 == parity
            mine = jnp.where(inside, 1 - y % 2, y % 2)
            kept_terms = pick(pair, 1 - mine)
            kept_terms = kept_terms + flip(pick(pair, mine), "y", 4, 1)
            pairs = [
                (s * 4 + r, (3 - s) * 4 + r)
                for s in range(4)
                for r in range(4)
                if s // 2 != r % 2
            ]
            summed = kept_terms + lax.ppermute(kept_terms, ("y", "rep"), pairs)
        else:
            summed = lax.all_to_all(
                terms.reshape(4, 8, strip, TILE), "y", split_axis=0, concat_axis=0, tiled=True
            ).sum(axis=0)
        summed, factors = tie((summed, factors))
        pieces = lax.all_to_all(
            summed, ("zh", "rep"), split_axis=0, concat_axis=0, tiled=True
        )
    chosen = pick(pieces.reshape(2, 2, 2, strip, TILE), y // 2, 2)
    scale = (2 * 64 * TILE) ** -0.5
    item_rhs = jnp.sum(chosen, axis=(0, 1)).T * (scale * STEP)
    return factors, item_rhs


def solution(mesh):
    fine = Mesh(np.asarray(mesh.devices).reshape(SIZES), AXES)
    rows = P(BLK, "rep")
    return jax.shard_map(
        per_device,
        mesh=fine,
        in_specs=(rows, rows, rows, P(BLK, "rep", None, None)),
        out_specs=(rows, rows),
        check_vma=False,
    )
```

```python
import functools

import jax
import jax.numpy as jnp
import numpy as np
from jax import lax
from jax.experimental import pallas as pl
from jax.experimental.pallas import tpu as pltpu
from jax.sharding import Mesh, PartitionSpec as P

ITERS = 2
AXES = ("y", "zh", "x", "core", "rep")
SIZES = (4, 2, 4, 2, 4)
BLK = ("y", "zh", "x", "core")
RANK = 256
TILE = 128
HALF = TILE // 2
GROUPS = 8
WIDE = 4 * TILE
RIDGE = 0.1
STEP = 0.1
f32 = jnp.float32
bf16 = jnp.bfloat16


def split(value):
    high = value.astype(bf16)
    low = (value - high.astype(f32)).astype(bf16)
    return high, low


def dot(a, b):
    return lax.dot_general(a, b, (((1,), (0,)), ((), ())), preferred_element_type=f32)


def dot_t(a, b):
    return lax.dot_general(a, b, (((1,), (1,)), ((), ())), preferred_element_type=f32)


def scores_of(stacked, panel_hi, panel_lo):
    both = dot(stacked, panel_hi)
    return both[:TILE] + both[TILE:] + dot(stacked[:TILE], panel_lo)


def project(mixed, panel_hi, panel_lo):
    high, low = split(mixed)
    both = dot_t(jnp.concatenate([high, low], axis=0), panel_hi)
    return both[:TILE] + both[TILE:] + dot_t(high, panel_lo)


def store_split(vectors, stacked):
    high, low = split(vectors)
    stacked[:TILE] = high
    stacked[TILE:] = low


def scores_kernel(
    x0_t, own, far, own_hi, own_lo, far_hi, far_lo, own_scores, far_scores, x0, stacked
):
    @pl.when(pl.program_id(0) == 0)
    def _():
        start = x0_t[...].T
        x0[...] = start
        store_split(start, stacked)

    sides = ((own, own_hi, own_lo, own_scores), (far, far_hi, far_lo, far_scores))
    for panels, hi, lo, scores in sides:
        for j in range(4):
            cols = slice(j * TILE, (j + 1) * TILE)
            high, low = split(panels[0, j])
            hi[0, :, cols] = high
            lo[0, :, cols] = low
        scores[0] = scores_of(stacked[...], hi[0], lo[0])


def first_kernel(scal, *refs):
    own_scores, far_scores, own_hi, own_lo, far_hi, far_lo, *refs = refs
    *refs, own_weight, far_weight, own_target, far_target, part = refs
    count = len(refs) // 2
    own_a, own_moved = refs[0], refs[1:count]
    far_a, far_moved = refs[count], refs[count + 1 :]
    i = pl.program_id(0)
    x, core = scal[2], scal[1]
    at = (lax.rem(x + 4 - i, 4) if REL else i) * 2

    @pl.when(i == 0)
    def _():
        part[...] = jnp.zeros_like(part)

    sides = (
        (core, own_scores, own_hi, own_lo, own_a, own_moved, own_weight, own_target),
        (1 - core, far_scores, far_hi, far_lo, far_a, far_moved, far_weight, far_target),
    )
    for which, scores, hi, lo, lev_a, moved, weight, target in sides:
        for j in range(4):
            cols = slice(j * TILE, (j + 1) * TILE)
            tile = j * GROUPS + at + which
            a1 = scal[3 + tile].astype(f32)
            b1 = scal[35 + tile].astype(f32)
            a0, b0 = 1.0 - a1, 1.0 - b1
            la = lev_a[j, 0, 0].astype(f32)
            lb = jnp.concatenate([rows[j, 0] for rows in moved], axis=0).astype(f32)
            ta = la + jnp.where(la > 0, 10.0, 0.0)
            tb = lb + jnp.where(lb > 0, 10.0, 0.0)
            weight[0, :HALF, cols] = (10.0 + a0 * la + b0 * lb).astype(bf16)
            weight[0, HALF:, cols] = (10.0 + a1 * la + b1 * lb).astype(bf16)
            target[0, :HALF, cols] = a0 * ta + b0 * tb
            target[0, HALF:, cols] = a1 * ta + b1 * tb
        mixed = STEP * (target[0] - weight[0].astype(f32) * scores[0])
        part[...] += project(mixed, hi[0], lo[0])


def apply_step(shared, part, stacked):
    own_hi, own_lo, far_hi, far_lo, own_weight, far_weight = shared
    for hi, lo, weight in ((own_hi, own_lo, own_weight), (far_hi, far_lo, far_weight)):
        scores = scores_of(stacked[...], hi[0], lo[0])
        mixed = STEP * (weight[0].astype(f32) * scores)
        part[...] += project(mixed, hi[0], lo[0])


def second_kernel(pa, pb, x0, *refs):
    shared, (resid, part, stacked) = refs[:6], refs[6:]

    @pl.when(pl.program_id(0) == 0)
    def _():
        start = pa[...] + pb[...] - RIDGE * x0[...]
        resid[...] = start
        store_split(start, stacked)
        part[...] = jnp.zeros_like(part)

    apply_step(shared, part, stacked)


def third_kernel(pa, pb, resid, x0, *refs):
    shared, (x1, resid1, direc1, part, stacked) = refs[:6], refs[6:]

    @pl.when(pl.program_id(0) == 0)
    def _():
        direc = resid[...]
        image = pa[...] + pb[...] + RIDGE * direc
        rho = jnp.sum(direc * direc, axis=1, keepdims=True)
        alpha = rho / jnp.sum(direc * image, axis=1, keepdims=True)
        x1[...] = x0[...] + alpha * direc
        after = direc - alpha * image
        resid1[...] = after
        rho_next = jnp.sum(after * after, axis=1, keepdims=True)
        ahead = after + (rho_next / rho) * direc
        direc1[...] = ahead
        store_split(ahead, stacked)
        part[...] = jnp.zeros_like(part)

    apply_step(shared, part, stacked)


def last_kernel(pa, pb, resid, direc, x1, out):
    image = pa[...] + pb[...] + RIDGE * direc[...]
    rho = jnp.sum(resid[...] * resid[...], axis=1, keepdims=True)
    alpha = rho / jnp.sum(direc[...] * image, axis=1, keepdims=True)
    out[...] = x1[...] + alpha * direc[...]


def rhs_kernel(own_vectors, far_vectors, own, got, t1, t2, t3, out, total):
    for k in range(4):
        for slot in range(2):
            chunk = (own_vectors, far_vectors)[slot][k]
            if slot == 1:
                tile = got[k]
            elif k == 0:
                tile = own[0]
            else:
                tile = (t1, t2, t3)[k - 1][0]
            tile = tile.astype(bf16)
            high, low = split(chunk.T)
            both = jnp.concatenate([high, low], axis=1)
            term = dot(both, jnp.concatenate([tile, tile], axis=0))
            if k == 0 and slot == 0:
                total[...] = term
            else:
                total[...] += term
    for j in range(4):
        out[0, j] = total[:, j * TILE : (j + 1) * TILE]
        out[1, j] = total[:, j * TILE : (j + 1) * TILE]


def spec(shape, index=None):
    if index is None:
        zeros = (0,) * len(shape)
        return pl.BlockSpec(shape, lambda *_: zeros)
    return pl.BlockSpec(shape, index)


def params():
    return pltpu.CompilerParams(vmem_limit_bytes=VMEM)


def cost(flops, moved):
    return pl.CostEstimate(flops=flops, bytes_accessed=moved, transcendentals=0)


APPLY_COST = 6 * 2 * TILE * GROUPS * WIDE * RANK


def shaped(*shape, dtype=f32):
    return jax.ShapeDtypeStruct(shape, dtype)


def group(*shape):
    return spec((1,) + shape, lambda i, *_: (i,) + (0,) * len(shape))


def first_scores(x0_t, own, far):
    half_panel = shaped(4, RANK, WIDE, dtype=bf16)
    return pl.pallas_call(
        scores_kernel,
        grid=(4,),
        in_specs=[spec((RANK, TILE))] + [group(4, RANK, TILE)] * 2,
        out_specs=[group(RANK, WIDE)] * 4 + [group(TILE, WIDE)] * 2 + [spec((TILE, RANK))],
        out_shape=[half_panel] * 4 + [shaped(4, TILE, WIDE)] * 2 + [shaped(TILE, RANK)],
        scratch_shapes=[pltpu.VMEM((2 * TILE, RANK), bf16)],
        compiler_params=params(),
        cost_estimate=cost(APPLY_COST // 2, 10 << 20),
        name="first_scores",
    )(x0_t, own, far)


def first_apply(scal, scores, panels, lev, moved):
    whole = (TILE, RANK)

    def side(i, s, far):
        return (lax.rem(s[2] + 4 - i, 4) if REL else i) * 2 + (1 - s[1] if far else s[1])

    levels_specs = []
    for far in (False, True):
        levels_specs += [
            spec((4, 1, 1, HALF, TILE), lambda i, s, far=far: (0, side(i, s, far), s[0], 0, 0)),
            *(
                spec((4, 1, n, TILE), lambda i, s, far=far: (0, side(i, s, far), 0, 0))
                for n in CHUNKS
            ),
        ]
    return pl.pallas_call(
        first_kernel,
        grid_spec=pltpu.PrefetchScalarGridSpec(
            num_scalar_prefetch=1,
            grid=(4,),
            in_specs=[group(TILE, WIDE)] * 2 + [group(RANK, WIDE)] * 4 + levels_specs,
            out_specs=[group(TILE, WIDE)] * 4 + [spec(whole)],
        ),
        out_shape=[shaped(4, TILE, WIDE, dtype=bf16)] * 2
        + [shaped(4, TILE, WIDE)] * 2
        + [shaped(*whole)],
        compiler_params=params(),
        cost_estimate=cost(APPLY_COST // 2, 12 << 20),
        name="first_apply",
    )(scal, *scores, *panels, lev, *moved, lev, *moved)


def next_apply(kernel, vectors, shared, outs, name):
    whole = (TILE, RANK)
    return pl.pallas_call(
        kernel,
        grid=(4,),
        in_specs=[spec(whole)] * len(vectors) + [group(RANK, WIDE)] * 4 + [group(TILE, WIDE)] * 2,
        out_specs=[spec(whole)] * outs,
        out_shape=[shaped(*whole)] * outs,
        scratch_shapes=[pltpu.VMEM((2 * TILE, RANK), bf16)],
        compiler_params=params(),
        cost_estimate=cost(APPLY_COST, 6 << 20),
        name=name,
    )(*vectors, *shared)


def shift(value, axis, size, by):
    return lax.ppermute(value, axis, [(i, (i + by) % size) for i in range(size)])


def flip(value, axis, size, bit):
    return lax.ppermute(value, axis, [(i, i ^ bit) for i in range(size)])


def pick(value, index, axis=0):
    return lax.dynamic_index_in_dim(value, index, axis, keepdims=False)


VMEM = 16777216
REL = 1
FP = 'early'
TAIL = 'a2a'
XC = 0
NP = 'y'
XS = 'perm'
CHUNKS = (56,8)
YS = 'a2a'


def everyone(value, axis, size):
    copies = jnp.broadcast_to(value[None], (size,) + value.shape)
    return lax.all_to_all(copies, axis, split_axis=0, concat_axis=0, tiled=True)


def along_y(value, move):
    pairs = [
        (s * 4 + r, move(s) * 4 + r) for s in range(4) for r in range(4) if s // 2 == r % 2
    ]
    return lax.ppermute(value, ("y", "rep"), pairs)


def per_device(factors_in, items, tile_user, levels):
    y, zh, x, core, rep = (lax.axis_index(name) for name in AXES)
    half, parity = rep // 2, rep % 2
    inside = y // 2 == parity
    strip = RANK // 4
    tie = lax.optimization_barrier

    lev = levels[0].reshape(32, 2, HALF, TILE)
    other = pick(lev, 1 - half, 1)
    parts, at = [], 0
    for rows in CHUNKS:
        parts.append(other[:, at : at + rows])
        at += rows
    users = factors_in.T.reshape(strip, 2, TILE)
    kept = lax.dynamic_slice_in_dim(users, half * HALF, HALF, 2).reshape(strip, TILE)
    given = lax.dynamic_slice_in_dim(users, (1 - half) * HALF, HALF, 2).reshape(strip, TILE)
    blocks = jnp.zeros((8, TILE), f32).at[0, :32].set(tile_user[0].astype(f32))
    given = jnp.concatenate([given, blocks])

    moved_levels = []
    got = flip(given, "rep", 4, 2)
    low = jnp.where(half == 0, kept, got[:strip])
    high = jnp.where(half == 0, got[:strip], kept)
    pair = jnp.stack([low, high])
    next_pair = flip(pair, "rep", 4, 1)
    panel = everyone(items.T, ("zh", "rep"), 8).reshape(2, RANK, TILE)
    if NP == "z":
        panel, pair, next_pair, got, *parts = tie((panel, pair, next_pair, got, *parts))
    else:
        panel, pair, got, *parts = tie((panel, pair, got, *parts))
        next_pair = flip(pair, "rep", 4, 1)

    moved_levels.append(flip(parts[0], "rep", 4, 2))
    if YS == "perm":
        inside = y // 2 == parity
        beside = along_y(panel, lambda s: s ^ 1)
        across = along_y(panel, lambda s: 3 - s)
        beyond = along_y(panel, lambda s: (s + 2) % 4)
        same = jnp.where(inside, panel, beyond)
        odd = jnp.where(inside, beside, across)
        even = y % 2 == 0
        panel = jnp.stack([jnp.where(even, same, odd), jnp.where(even, odd, same)])
    elif YS == "two":
        inside = y // 2 == parity
        across = along_y(panel, lambda s: 3 - s)
        now = jnp.where(inside, panel, across)
        beside = flip(now, "y", 4, 1)
        even = (y % 2 == 0) == inside
        panel = jnp.stack([jnp.where(even, now, beside), jnp.where(even, beside, now)])
    else:
        panel = everyone(panel, "y", 4).reshape(4, 2, RANK, TILE)
        panel = lax.dynamic_slice_in_dim(panel, 2 * parity, 2, 0)
    panel = panel.reshape(4, RANK, TILE)
    panel, pair, got, *parts = tie((panel, pair, got, *parts[1:]))

    if XC:
        moved_levels.append(flip(parts[0], "rep", 4, 2))
        parts = parts[1:]
    if XS == "ring":
        left, right = shift(panel, "x", 4, 1), shift(panel, "x", 4, -1)
        over = jnp.concatenate([shift(left[:2], "x", 4, 1), shift(right[2:], "x", 4, -1)])
        own_panels = jnp.stack([panel, left, over, right])
    elif XS == "perm":
        own_panels = jnp.stack([panel] + [shift(panel, "x", 4, k) for k in (1, 2, 3)])
    else:
        own_panels = everyone(panel, "x", 4).reshape(4, 4, RANK, TILE)
    own_panels, pair, next_pair, got, moved_levels, *parts = tie(
        (own_panels, pair, next_pair, got, moved_levels, *parts)
    )
    moved_levels = moved_levels + [flip(rows, "rep", 4, 2) for rows in parts]
    far_panels = flip(own_panels, "core", 2, 1)
    user_b = got[strip, :32].astype(jnp.int32)
    place = jnp.stack([half, core, x]).astype(jnp.int32)
    scal = jnp.concatenate([place, tile_user[0], user_b])
    first = jnp.where(parity == 0, pair, next_pair)
    second = jnp.where(parity == 0, next_pair, pair)
    x0_t = jnp.stack([first, second], axis=1).reshape(RANK, TILE)

    *panels, own_scores, far_scores, x0 = first_scores(x0_t, own_panels, far_panels)
    *weights, target, far_target, part = first_apply(
        scal,
        (own_scores, far_scores),
        panels,
        lev.reshape(4, GROUPS, 2, HALF, TILE),
        [rows.reshape(4, GROUPS, -1, TILE) for rows in moved_levels],
    )
    shared = (*panels, *weights)
    part_b = flip(part, "rep", 4, 1)

    moved = [shift(jnp.stack([target[k], far_target[k]]), "x", 4, -k) for k in (1, 2, 3)]

    resid, part = next_apply(second_kernel, (part, part_b, x0), shared, 2, "second_apply")
    part_b = flip(part, "rep", 4, 1)
    x1, resid1, direc1, part = next_apply(
        third_kernel, (part, part_b, resid, x0), shared, 4, "third_apply"
    )
    part_b = flip(part, "rep", 4, 1)
    part_b, moved = tie((part_b, moved))
    got = flip(jnp.stack([far_target[0]] + [v[1] for v in moved]), "core", 2, 1)
    solved = pl.pallas_call(
        last_kernel,
        out_shape=shaped(TILE, RANK),
        compiler_params=params(),
        cost_estimate=cost(TILE * RANK * 10, 6 * TILE * RANK * 4),
        name="last_update",
    )(part, part_b, resid1, direc1, x1)

    vectors = jnp.stack([solved] + [shift(solved, "x", 4, -k) for k in (1, 2, 3)])
    far_vectors = flip(vectors, "core", 2, 1)

    vmem = pl.BlockSpec(memory_space=pltpu.VMEM)
    terms = pl.pallas_call(
        rhs_kernel,
        in_specs=[vmem] * 7,
        out_shape=shaped(2, 4, RANK, TILE),
        scratch_shapes=[pltpu.VMEM((RANK, WIDE), f32)],
        compiler_params=params(),
        cost_estimate=cost(4 * 1024 * RANK * WIDE, 4 << 20),
        name="rhs_terms",
    )(vectors, far_vectors, target, got, *moved)

    if FP == 'late':
        terms, solved = tie((terms, solved))
    strips = solved.reshape(TILE, 4, strip)
    sent = flip(pick(strips, rep ^ 2, 1), "rep", 4, 2)
    kept = pick(strips, rep, 1)
    low = jnp.where(half == 0, kept, sent).reshape(2, HALF, strip)
    high = jnp.where(half == 0, sent, kept).reshape(2, HALF, strip)
    factors = jnp.stack([low, high], axis=1).reshape(2 * TILE, strip)

    if TAIL == "one":
        pieces = lax.all_to_all(
            terms.reshape(32, strip, TILE),
            ("y", "zh", "rep"),
            split_axis=0,
            concat_axis=0,
            tiled=True,
        )
        pieces = pieces.reshape(4, 8, strip, TILE).sum(axis=0)
    else:
        if TAIL == "two":
            pair = terms.reshape(4, 8, strip, TILE)
            inside = y // 2 == parity
            mine = jnp.where(inside, 1 - y % 2, y % 2)
            kept_terms = pick(pair, 1 - mine)
            kept_terms = kept_terms + flip(pick(pair, mine), "y", 4, 1)
            pairs = [
                (s * 4 + r, (3 - s) * 4 + r)
                for s in range(4)
                for r in range(4)
                if s // 2 != r % 2
            ]
            summed = kept_terms + lax.ppermute(kept_terms, ("y", "rep"), pairs)
        else:
            summed = lax.all_to_all(
                terms.reshape(4, 8, strip, TILE), "y", split_axis=0, concat_axis=0, tiled=True
            ).sum(axis=0)
        summed, factors = tie((summed, factors))
        pieces = lax.all_to_all(
            summed, ("zh", "rep"), split_axis=0, concat_axis=0, tiled=True
        )
    chosen = pick(pieces.reshape(2, 2, 2, strip, TILE), y // 2, 2)
    scale = (2 * 64 * TILE) ** -0.5
    item_rhs = jnp.sum(chosen, axis=(0, 1)).T * (scale * STEP)
    return factors, item_rhs


def solution(mesh):
    fine = Mesh(np.asarray(mesh.devices).reshape(SIZES), AXES)
    rows = P(BLK, "rep")
    return jax.shard_map(
        per_device,
        mesh=fine,
        in_specs=(rows, rows, rows, P(BLK, "rep", None, None)),
        out_specs=(rows, rows),
        check_vma=False,
    )
```

```python
import functools

import jax
import jax.numpy as jnp
import numpy as np
from jax import lax
from jax.experimental import pallas as pl
from jax.experimental.pallas import tpu as pltpu
from jax.sharding import Mesh, PartitionSpec as P

ITERS = 2
AXES = ("y", "zh", "x", "core", "rep")
SIZES = (4, 2, 4, 2, 4)
BLK = ("y", "zh", "x", "core")
RANK = 256
TILE = 128
HALF = TILE // 2
GROUPS = 8
WIDE = 4 * TILE
RIDGE = 0.1
STEP = 0.1
f32 = jnp.float32
bf16 = jnp.bfloat16


def split(value):
    high = value.astype(bf16)
    low = (value - high.astype(f32)).astype(bf16)
    return high, low


def dot(a, b):
    return lax.dot_general(a, b, (((1,), (0,)), ((), ())), preferred_element_type=f32)


def dot_t(a, b):
    return lax.dot_general(a, b, (((1,), (1,)), ((), ())), preferred_element_type=f32)


def scores_of(stacked, panel_hi, panel_lo):
    both = dot(stacked, panel_hi)
    return both[:TILE] + both[TILE:] + dot(stacked[:TILE], panel_lo)


def project(mixed, panel_hi, panel_lo):
    high, low = split(mixed)
    both = dot_t(jnp.concatenate([high, low], axis=0), panel_hi)
    return both[:TILE] + both[TILE:] + dot_t(high, panel_lo)


def store_split(vectors, stacked):
    high, low = split(vectors)
    stacked[:TILE] = high
    stacked[TILE:] = low


def scores_kernel(
    x0_t, own, far, own_hi, own_lo, far_hi, far_lo, own_scores, far_scores, x0, stacked
):
    @pl.when(pl.program_id(0) == 0)
    def _():
        start = x0_t[...].T
        x0[...] = start
        store_split(start, stacked)

    sides = ((own, own_hi, own_lo, own_scores), (far, far_hi, far_lo, far_scores))
    for panels, hi, lo, scores in sides:
        for j in range(4):
            cols = slice(j * TILE, (j + 1) * TILE)
            high, low = split(panels[0, j])
            hi[0, :, cols] = high
            lo[0, :, cols] = low
        scores[0] = scores_of(stacked[...], hi[0], lo[0])


def first_kernel(scal, *refs):
    own_scores, far_scores, own_hi, own_lo, far_hi, far_lo, *refs = refs
    *refs, own_weight, far_weight, own_target, far_target, part = refs
    count = len(refs) // 2
    own_a, own_moved = refs[0], refs[1:count]
    far_a, far_moved = refs[count], refs[count + 1 :]
    i = pl.program_id(0)
    x, core = scal[2], scal[1]
    at = (lax.rem(x + 4 - i, 4) if REL else i) * 2

    @pl.when(i == 0)
    def _():
        part[...] = jnp.zeros_like(part)

    sides = (
        (core, own_scores, own_hi, own_lo, own_a, own_moved, own_weight, own_target),
        (1 - core, far_scores, far_hi, far_lo, far_a, far_moved, far_weight, far_target),
    )
    for which, scores, hi, lo, lev_a, moved, weight, target in sides:
        for j in range(4):
            cols = slice(j * TILE, (j + 1) * TILE)
            tile = j * GROUPS + at + which
            a1 = scal[3 + tile].astype(f32)
            b1 = scal[35 + tile].astype(f32)
            a0, b0 = 1.0 - a1, 1.0 - b1
            la = lev_a[j, 0, 0].astype(f32)
            lb = jnp.concatenate([rows[j, 0] for rows in moved], axis=0).astype(f32)
            ta = la + jnp.where(la > 0, 10.0, 0.0)
            tb = lb + jnp.where(lb > 0, 10.0, 0.0)
            weight[0, :HALF, cols] = (10.0 + a0 * la + b0 * lb).astype(bf16)
            weight[0, HALF:, cols] = (10.0 + a1 * la + b1 * lb).astype(bf16)
            target[0, :HALF, cols] = a0 * ta + b0 * tb
            target[0, HALF:, cols] = a1 * ta + b1 * tb
        mixed = STEP * (target[0] - weight[0].astype(f32) * scores[0])
        part[...] += project(mixed, hi[0], lo[0])


def apply_step(shared, part, stacked):
    own_hi, own_lo, far_hi, far_lo, own_weight, far_weight = shared
    for hi, lo, weight in ((own_hi, own_lo, own_weight), (far_hi, far_lo, far_weight)):
        scores = scores_of(stacked[...], hi[0], lo[0])
        mixed = STEP * (weight[0].astype(f32) * scores)
        part[...] += project(mixed, hi[0], lo[0])


def second_kernel(pa, pb, x0, *refs):
    shared, (resid, part, stacked) = refs[:6], refs[6:]

    @pl.when(pl.program_id(0) == 0)
    def _():
        start = pa[...] + pb[...] - RIDGE * x0[...]
        resid[...] = start
        store_split(start, stacked)
        part[...] = jnp.zeros_like(part)

    apply_step(shared, part, stacked)


def third_kernel(pa, pb, resid, x0, *refs):
    shared, (x1, resid1, direc1, part, stacked) = refs[:6], refs[6:]

    @pl.when(pl.program_id(0) == 0)
    def _():
        direc = resid[...]
        image = pa[...] + pb[...] + RIDGE * direc
        rho = jnp.sum(direc * direc, axis=1, keepdims=True)
        alpha = rho / jnp.sum(direc * image, axis=1, keepdims=True)
        x1[...] = x0[...] + alpha * direc
        after = direc - alpha * image
        resid1[...] = after
        rho_next = jnp.sum(after * after, axis=1, keepdims=True)
        ahead = after + (rho_next / rho) * direc
        direc1[...] = ahead
        store_split(ahead, stacked)
        part[...] = jnp.zeros_like(part)

    apply_step(shared, part, stacked)


def last_kernel(pa, pb, resid, direc, x1, out):
    image = pa[...] + pb[...] + RIDGE * direc[...]
    rho = jnp.sum(resid[...] * resid[...], axis=1, keepdims=True)
    alpha = rho / jnp.sum(direc[...] * image, axis=1, keepdims=True)
    out[...] = x1[...] + alpha * direc[...]


def rhs_kernel(own_vectors, far_vectors, own, got, t1, t2, t3, out, total):
    for k in range(4):
        for slot in range(2):
            chunk = (own_vectors, far_vectors)[slot][k]
            if slot == 1:
                tile = got[k]
            elif k == 0:
                tile = own[0]
            else:
                tile = (t1, t2, t3)[k - 1][0]
            tile = tile.astype(bf16)
            high, low = split(chunk.T)
            both = jnp.concatenate([high, low], axis=1)
            term = dot(both, jnp.concatenate([tile, tile], axis=0))
            if k == 0 and slot == 0:
                total[...] = term
            else:
                total[...] += term
    for j in range(4):
        out[0, j] = total[:, j * TILE : (j + 1) * TILE]
        out[1, j] = total[:, j * TILE : (j + 1) * TILE]


def spec(shape, index=None):
    if index is None:
        zeros = (0,) * len(shape)
        return pl.BlockSpec(shape, lambda *_: zeros)
    return pl.BlockSpec(shape, index)


def params():
    return pltpu.CompilerParams(vmem_limit_bytes=VMEM)


def cost(flops, moved):
    return pl.CostEstimate(flops=flops, bytes_accessed=moved, transcendentals=0)


APPLY_COST = 6 * 2 * TILE * GROUPS * WIDE * RANK


def shaped(*shape, dtype=f32):
    return jax.ShapeDtypeStruct(shape, dtype)


def group(*shape):
    return spec((1,) + shape, lambda i, *_: (i,) + (0,) * len(shape))


def first_scores(x0_t, own, far):
    half_panel = shaped(4, RANK, WIDE, dtype=bf16)
    return pl.pallas_call(
        scores_kernel,
        grid=(4,),
        in_specs=[spec((RANK, TILE))] + [group(4, RANK, TILE)] * 2,
        out_specs=[group(RANK, WIDE)] * 4 + [group(TILE, WIDE)] * 2 + [spec((TILE, RANK))],
        out_shape=[half_panel] * 4 + [shaped(4, TILE, WIDE)] * 2 + [shaped(TILE, RANK)],
        scratch_shapes=[pltpu.VMEM((2 * TILE, RANK), bf16)],
        compiler_params=params(),
        cost_estimate=cost(APPLY_COST // 2, 10 << 20),
        name="first_scores",
    )(x0_t, own, far)


def first_apply(scal, scores, panels, lev, moved):
    whole = (TILE, RANK)

    def side(i, s, far):
        return (lax.rem(s[2] + 4 - i, 4) if REL else i) * 2 + (1 - s[1] if far else s[1])

    levels_specs = []
    for far in (False, True):
        levels_specs += [
            spec((4, 1, 1, HALF, TILE), lambda i, s, far=far: (0, side(i, s, far), s[0], 0, 0)),
            *(
                spec((4, 1, n, TILE), lambda i, s, far=far: (0, side(i, s, far), 0, 0))
                for n in CHUNKS
            ),
        ]
    return pl.pallas_call(
        first_kernel,
        grid_spec=pltpu.PrefetchScalarGridSpec(
            num_scalar_prefetch=1,
            grid=(4,),
            in_specs=[group(TILE, WIDE)] * 2 + [group(RANK, WIDE)] * 4 + levels_specs,
            out_specs=[group(TILE, WIDE)] * 4 + [spec(whole)],
        ),
        out_shape=[shaped(4, TILE, WIDE, dtype=bf16)] * 2
        + [shaped(4, TILE, WIDE)] * 2
        + [shaped(*whole)],
        compiler_params=params(),
        cost_estimate=cost(APPLY_COST // 2, 12 << 20),
        name="first_apply",
    )(scal, *scores, *panels, lev, *moved, lev, *moved)


def next_apply(kernel, vectors, shared, outs, name):
    whole = (TILE, RANK)
    return pl.pallas_call(
        kernel,
        grid=(4,),
        in_specs=[spec(whole)] * len(vectors) + [group(RANK, WIDE)] * 4 + [group(TILE, WIDE)] * 2,
        out_specs=[spec(whole)] * outs,
        out_shape=[shaped(*whole)] * outs,
        scratch_shapes=[pltpu.VMEM((2 * TILE, RANK), bf16)],
        compiler_params=params(),
        cost_estimate=cost(APPLY_COST, 6 << 20),
        name=name,
    )(*vectors, *shared)


def shift(value, axis, size, by):
    return lax.ppermute(value, axis, [(i, (i + by) % size) for i in range(size)])


def flip(value, axis, size, bit):
    return lax.ppermute(value, axis, [(i, i ^ bit) for i in range(size)])


def pick(value, index, axis=0):
    return lax.dynamic_index_in_dim(value, index, axis, keepdims=False)


VMEM = 16777216
REL = 1
FP = 'early'
TAIL = 'a2a'
XC = 0
NP = 'y'
XS = 'perm'
CHUNKS = (56,8)
YS = 'perm'
DT = 'after'


def everyone(value, axis, size):
    copies = jnp.broadcast_to(value[None], (size,) + value.shape)
    return lax.all_to_all(copies, axis, split_axis=0, concat_axis=0, tiled=True)


def along_y(value, move):
    pairs = [
        (s * 4 + r, move(s) * 4 + r) for s in range(4) for r in range(4) if s // 2 == r % 2
    ]
    return lax.ppermute(value, ("y", "rep"), pairs)


def per_device(factors_in, items, tile_user, levels):
    y, zh, x, core, rep = (lax.axis_index(name) for name in AXES)
    half, parity = rep // 2, rep % 2
    inside = y // 2 == parity
    strip = RANK // 4
    tie = lax.optimization_barrier

    lev = levels[0].reshape(32, 2, HALF, TILE)
    other = pick(lev, 1 - half, 1)
    parts, at = [], 0
    for rows in CHUNKS:
        parts.append(other[:, at : at + rows])
        at += rows
    users = factors_in.T.reshape(strip, 2, TILE)
    kept = lax.dynamic_slice_in_dim(users, half * HALF, HALF, 2).reshape(strip, TILE)
    given = lax.dynamic_slice_in_dim(users, (1 - half) * HALF, HALF, 2).reshape(strip, TILE)
    blocks = jnp.zeros((8, TILE), f32).at[0, :32].set(tile_user[0].astype(f32))
    given = jnp.concatenate([given, blocks])

    moved_levels = []
    got = flip(given, "rep", 4, 2)
    low = jnp.where(half == 0, kept, got[:strip])
    high = jnp.where(half == 0, got[:strip], kept)
    pair = jnp.stack([low, high])
    next_pair = flip(pair, "rep", 4, 1)
    panel = everyone(items.T, ("zh", "rep"), 8).reshape(2, RANK, TILE)
    if NP == "z":
        panel, pair, next_pair, got, *parts = tie((panel, pair, next_pair, got, *parts))
    else:
        panel, pair, got, *parts = tie((panel, pair, got, *parts))
        next_pair = flip(pair, "rep", 4, 1)

    moved_levels.append(flip(parts[0], "rep", 4, 2))
    if YS == "perm":
        inside = y // 2 == parity
        beside = along_y(panel, lambda s: s ^ 1)
        across = along_y(panel, lambda s: 3 - s)
        beyond = along_y(panel, lambda s: (s + 2) % 4)
        same = jnp.where(inside, panel, beyond)
        odd = jnp.where(inside, beside, across)
        even = y % 2 == 0
        panel = jnp.stack([jnp.where(even, same, odd), jnp.where(even, odd, same)])
    elif YS == "two":
        inside = y // 2 == parity
        across = along_y(panel, lambda s: 3 - s)
        now = jnp.where(inside, panel, across)
        beside = flip(now, "y", 4, 1)
        even = (y % 2 == 0) == inside
        panel = jnp.stack([jnp.where(even, now, beside), jnp.where(even, beside, now)])
    else:
        panel = everyone(panel, "y", 4).reshape(4, 2, RANK, TILE)
        panel = lax.dynamic_slice_in_dim(panel, 2 * parity, 2, 0)
    panel = panel.reshape(4, RANK, TILE)
    panel, pair, got, *parts = tie((panel, pair, got, *parts[1:]))

    if XC:
        moved_levels.append(flip(parts[0], "rep", 4, 2))
        parts = parts[1:]
    if XS == "ring":
        left, right = shift(panel, "x", 4, 1), shift(panel, "x", 4, -1)
        over = jnp.concatenate([shift(left[:2], "x", 4, 1), shift(right[2:], "x", 4, -1)])
        own_panels = jnp.stack([panel, left, over, right])
    elif XS == "perm":
        own_panels = jnp.stack([panel] + [shift(panel, "x", 4, k) for k in (1, 2, 3)])
    else:
        own_panels = everyone(panel, "x", 4).reshape(4, 4, RANK, TILE)
    own_panels, pair, next_pair, got, moved_levels, *parts = tie(
        (own_panels, pair, next_pair, got, moved_levels, *parts)
    )
    moved_levels = moved_levels + [flip(rows, "rep", 4, 2) for rows in parts]
    far_panels = flip(own_panels, "core", 2, 1)
    user_b = got[strip, :32].astype(jnp.int32)
    place = jnp.stack([half, core, x]).astype(jnp.int32)
    scal = jnp.concatenate([place, tile_user[0], user_b])
    first = jnp.where(parity == 0, pair, next_pair)
    second = jnp.where(parity == 0, next_pair, pair)
    x0_t = jnp.stack([first, second], axis=1).reshape(RANK, TILE)

    *panels, own_scores, far_scores, x0 = first_scores(x0_t, own_panels, far_panels)
    *weights, target, far_target, part = first_apply(
        scal,
        (own_scores, far_scores),
        panels,
        lev.reshape(4, GROUPS, 2, HALF, TILE),
        [rows.reshape(4, GROUPS, -1, TILE) for rows in moved_levels],
    )
    shared = (*panels, *weights)
    part_b = flip(part, "rep", 4, 1)

    moved = [shift(jnp.stack([target[k], far_target[k]]), "x", 4, -k) for k in (1, 2, 3)]

    resid, part = next_apply(second_kernel, (part, part_b, x0), shared, 2, "second_apply")
    part_b = flip(part, "rep", 4, 1)
    x1, resid1, direc1, part = next_apply(
        third_kernel, (part, part_b, resid, x0), shared, 4, "third_apply"
    )
    part_b = flip(part, "rep", 4, 1)
    solved = pl.pallas_call(
        last_kernel,
        out_shape=shaped(TILE, RANK),
        compiler_params=params(),
        cost_estimate=cost(TILE * RANK * 10, 6 * TILE * RANK * 4),
        name="last_update",
    )(part, part_b, resid1, direc1, x1)

    vectors = [shift(solved, "x", 4, -k) for k in (1, 2, 3)]
    if DT == "after":
        vectors, moved = tie((vectors, moved))
    else:
        solved, moved = tie((solved, moved))
    got = flip(jnp.stack([far_target[0]] + [v[1] for v in moved]), "core", 2, 1)
    vectors = jnp.stack([solved] + vectors)
    far_vectors = flip(vectors, "core", 2, 1)

    vmem = pl.BlockSpec(memory_space=pltpu.VMEM)
    terms = pl.pallas_call(
        rhs_kernel,
        in_specs=[vmem] * 7,
        out_shape=shaped(2, 4, RANK, TILE),
        scratch_shapes=[pltpu.VMEM((RANK, WIDE), f32)],
        compiler_params=params(),
        cost_estimate=cost(4 * 1024 * RANK * WIDE, 4 << 20),
        name="rhs_terms",
    )(vectors, far_vectors, target, got, *moved)

    if FP == 'late':
        terms, solved = tie((terms, solved))
    strips = solved.reshape(TILE, 4, strip)
    sent = flip(pick(strips, rep ^ 2, 1), "rep", 4, 2)
    kept = pick(strips, rep, 1)
    low = jnp.where(half == 0, kept, sent).reshape(2, HALF, strip)
    high = jnp.where(half == 0, sent, kept).reshape(2, HALF, strip)
    factors = jnp.stack([low, high], axis=1).reshape(2 * TILE, strip)

    if TAIL == "one":
        pieces = lax.all_to_all(
            terms.reshape(32, strip, TILE),
            ("y", "zh", "rep"),
            split_axis=0,
            concat_axis=0,
            tiled=True,
        )
        pieces = pieces.reshape(4, 8, strip, TILE).sum(axis=0)
    else:
        if TAIL == "two":
            pair = terms.reshape(4, 8, strip, TILE)
            inside = y // 2 == parity
            mine = jnp.where(inside, 1 - y % 2, y % 2)
            kept_terms = pick(pair, 1 - mine)
            kept_terms = kept_terms + flip(pick(pair, mine), "y", 4, 1)
            pairs = [
                (s * 4 + r, (3 - s) * 4 + r)
                for s in range(4)
                for r in range(4)
                if s // 2 != r % 2
            ]
            summed = kept_terms + lax.ppermute(kept_terms, ("y", "rep"), pairs)
        else:
            summed = lax.all_to_all(
                terms.reshape(4, 8, strip, TILE), "y", split_axis=0, concat_axis=0, tiled=True
            ).sum(axis=0)
        summed, factors = tie((summed, factors))
        pieces = lax.all_to_all(
            summed, ("zh", "rep"), split_axis=0, concat_axis=0, tiled=True
        )
    chosen = pick(pieces.reshape(2, 2, 2, strip, TILE), y // 2, 2)
    scale = (2 * 64 * TILE) ** -0.5
    item_rhs = jnp.sum(chosen, axis=(0, 1)).T * (scale * STEP)
    return factors, item_rhs


def solution(mesh):
    fine = Mesh(np.asarray(mesh.devices).reshape(SIZES), AXES)
    rows = P(BLK, "rep")
    return jax.shard_map(
        per_device,
        mesh=fine,
        in_specs=(rows, rows, rows, P(BLK, "rep", None, None)),
        out_specs=(rows, rows),
        check_vma=False,
    )
```

```python
import functools

import jax
import jax.numpy as jnp
import numpy as np
from jax import lax
from jax.experimental import pallas as pl
from jax.experimental.pallas import tpu as pltpu
from jax.sharding import Mesh, PartitionSpec as P

ITERS = 2
AXES = ("y", "zh", "x", "core", "rep")
SIZES = (4, 2, 4, 2, 4)
BLK = ("y", "zh", "x", "core")
RANK = 256
TILE = 128
HALF = TILE // 2
GROUPS = 8
WIDE = 4 * TILE
RIDGE = 0.1
STEP = 0.1
f32 = jnp.float32
bf16 = jnp.bfloat16


def split(value):
    high = value.astype(bf16)
    low = (value - high.astype(f32)).astype(bf16)
    return high, low


def dot(a, b):
    return lax.dot_general(a, b, (((1,), (0,)), ((), ())), preferred_element_type=f32)


def dot_t(a, b):
    return lax.dot_general(a, b, (((1,), (1,)), ((), ())), preferred_element_type=f32)


def scores_of(stacked, panel_hi, panel_lo):
    both = dot(stacked, panel_hi)
    return both[:TILE] + both[TILE:] + dot(stacked[:TILE], panel_lo)


def project(mixed, panel_hi, panel_lo):
    high, low = split(mixed)
    both = dot_t(jnp.concatenate([high, low], axis=0), panel_hi)
    return both[:TILE] + both[TILE:] + dot_t(high, panel_lo)


def store_split(vectors, stacked):
    high, low = split(vectors)
    stacked[:TILE] = high
    stacked[TILE:] = low


def scores_kernel(
    x0_t, own, far, own_hi, own_lo, far_hi, far_lo, own_scores, far_scores, x0, stacked
):
    @pl.when(pl.program_id(0) == 0)
    def _():
        start = x0_t[...].T
        x0[...] = start
        store_split(start, stacked)

    sides = ((own, own_hi, own_lo, own_scores), (far, far_hi, far_lo, far_scores))
    for panels, hi, lo, scores in sides:
        for j in range(4):
            cols = slice(j * TILE, (j + 1) * TILE)
            high, low = split(panels[0, j])
            hi[0, :, cols] = high
            lo[0, :, cols] = low
        scores[0] = scores_of(stacked[...], hi[0], lo[0])


def first_kernel(scal, *refs):
    own_scores, far_scores, own_hi, own_lo, far_hi, far_lo, *refs = refs
    *refs, own_weight, far_weight, own_target, far_target, part = refs
    count = len(refs) // 2
    own_a, own_moved = refs[0], refs[1:count]
    far_a, far_moved = refs[count], refs[count + 1 :]
    i = pl.program_id(0)
    x, core = scal[2], scal[1]
    at = (lax.rem(x + 4 - i, 4) if REL else i) * 2

    @pl.when(i == 0)
    def _():
        part[...] = jnp.zeros_like(part)

    sides = (
        (core, own_scores, own_hi, own_lo, own_a, own_moved, own_weight, own_target),
        (1 - core, far_scores, far_hi, far_lo, far_a, far_moved, far_weight, far_target),
    )
    for which, scores, hi, lo, lev_a, moved, weight, target in sides:
        for j in range(4):
            cols = slice(j * TILE, (j + 1) * TILE)
            tile = j * GROUPS + at + which
            a1 = scal[3 + tile].astype(f32)
            b1 = scal[35 + tile].astype(f32)
            a0, b0 = 1.0 - a1, 1.0 - b1
            la = lev_a[j, 0, 0].astype(f32)
            lb = jnp.concatenate([rows[j, 0] for rows in moved], axis=0).astype(f32)
            ta = la + jnp.where(la > 0, 10.0, 0.0)
            tb = lb + jnp.where(lb > 0, 10.0, 0.0)
            weight[0, :HALF, cols] = (10.0 + a0 * la + b0 * lb).astype(bf16)
            weight[0, HALF:, cols] = (10.0 + a1 * la + b1 * lb).astype(bf16)
            target[0, :HALF, cols] = a0 * ta + b0 * tb
            target[0, HALF:, cols] = a1 * ta + b1 * tb
        mixed = STEP * (target[0] - weight[0].astype(f32) * scores[0])
        part[...] += project(mixed, hi[0], lo[0])


def apply_step(shared, part, stacked):
    own_hi, own_lo, far_hi, far_lo, own_weight, far_weight = shared
    for hi, lo, weight in ((own_hi, own_lo, own_weight), (far_hi, far_lo, far_weight)):
        scores = scores_of(stacked[...], hi[0], lo[0])
        mixed = STEP * (weight[0].astype(f32) * scores)
        part[...] += project(mixed, hi[0], lo[0])


def second_kernel(pa, pb, x0, *refs):
    shared, (resid, part, stacked) = refs[:6], refs[6:]

    @pl.when(pl.program_id(0) == 0)
    def _():
        start = pa[...] + pb[...] - RIDGE * x0[...]
        resid[...] = start
        store_split(start, stacked)
        part[...] = jnp.zeros_like(part)

    apply_step(shared, part, stacked)


def third_kernel(pa, pb, resid, x0, *refs):
    shared, (x1, resid1, direc1, part, stacked) = refs[:6], refs[6:]

    @pl.when(pl.program_id(0) == 0)
    def _():
        direc = resid[...]
        image = pa[...] + pb[...] + RIDGE * direc
        rho = jnp.sum(direc * direc, axis=1, keepdims=True)
        alpha = rho / jnp.sum(direc * image, axis=1, keepdims=True)
        x1[...] = x0[...] + alpha * direc
        after = direc - alpha * image
        resid1[...] = after
        rho_next = jnp.sum(after * after, axis=1, keepdims=True)
        ahead = after + (rho_next / rho) * direc
        direc1[...] = ahead
        store_split(ahead, stacked)
        part[...] = jnp.zeros_like(part)

    apply_step(shared, part, stacked)


def last_kernel(pa, pb, resid, direc, x1, out):
    image = pa[...] + pb[...] + RIDGE * direc[...]
    rho = jnp.sum(resid[...] * resid[...], axis=1, keepdims=True)
    alpha = rho / jnp.sum(direc[...] * image, axis=1, keepdims=True)
    out[...] = x1[...] + alpha * direc[...]


def rhs_kernel(own_vectors, far_vectors, own, got, t1, t2, t3, out, total):
    for k in range(4):
        for slot in range(2):
            chunk = (own_vectors, far_vectors)[slot][k]
            if slot == 1:
                tile = got[k]
            elif k == 0:
                tile = own[0]
            else:
                tile = (t1, t2, t3)[k - 1][0]
            tile = tile.astype(bf16)
            high, low = split(chunk.T)
            both = jnp.concatenate([high, low], axis=1)
            term = dot(both, jnp.concatenate([tile, tile], axis=0))
            if k == 0 and slot == 0:
                total[...] = term
            else:
                total[...] += term
    for j in range(4):
        out[0, j] = total[:, j * TILE : (j + 1) * TILE]
        out[1, j] = total[:, j * TILE : (j + 1) * TILE]


def spec(shape, index=None):
    if index is None:
        zeros = (0,) * len(shape)
        return pl.BlockSpec(shape, lambda *_: zeros)
    return pl.BlockSpec(shape, index)


def params():
    return pltpu.CompilerParams(vmem_limit_bytes=VMEM)


def cost(flops, moved):
    return pl.CostEstimate(flops=flops, bytes_accessed=moved, transcendentals=0)


APPLY_COST = 6 * 2 * TILE * GROUPS * WIDE * RANK


def shaped(*shape, dtype=f32):
    return jax.ShapeDtypeStruct(shape, dtype)


def group(*shape):
    return spec((1,) + shape, lambda i, *_: (i,) + (0,) * len(shape))


def first_scores(x0_t, own, far):
    half_panel = shaped(4, RANK, WIDE, dtype=bf16)
    return pl.pallas_call(
        scores_kernel,
        grid=(4,),
        in_specs=[spec((RANK, TILE))] + [group(4, RANK, TILE)] * 2,
        out_specs=[group(RANK, WIDE)] * 4 + [group(TILE, WIDE)] * 2 + [spec((TILE, RANK))],
        out_shape=[half_panel] * 4 + [shaped(4, TILE, WIDE)] * 2 + [shaped(TILE, RANK)],
        scratch_shapes=[pltpu.VMEM((2 * TILE, RANK), bf16)],
        compiler_params=params(),
        cost_estimate=cost(APPLY_COST // 2, 10 << 20),
        name="first_scores",
    )(x0_t, own, far)


def first_apply(scal, scores, panels, lev, moved):
    whole = (TILE, RANK)

    def side(i, s, far):
        return (lax.rem(s[2] + 4 - i, 4) if REL else i) * 2 + (1 - s[1] if far else s[1])

    levels_specs = []
    for far in (False, True):
        levels_specs += [
            spec((4, 1, 1, HALF, TILE), lambda i, s, far=far: (0, side(i, s, far), s[0], 0, 0)),
            *(
                spec((4, 1, n, TILE), lambda i, s, far=far: (0, side(i, s, far), 0, 0))
                for n in CHUNKS
            ),
        ]
    return pl.pallas_call(
        first_kernel,
        grid_spec=pltpu.PrefetchScalarGridSpec(
            num_scalar_prefetch=1,
            grid=(4,),
            in_specs=[group(TILE, WIDE)] * 2 + [group(RANK, WIDE)] * 4 + levels_specs,
            out_specs=[group(TILE, WIDE)] * 4 + [spec(whole)],
        ),
        out_shape=[shaped(4, TILE, WIDE, dtype=bf16)] * 2
        + [shaped(4, TILE, WIDE)] * 2
        + [shaped(*whole)],
        compiler_params=params(),
        cost_estimate=cost(APPLY_COST // 2, 12 << 20),
        name="first_apply",
    )(scal, *scores, *panels, lev, *moved, lev, *moved)


def next_apply(kernel, vectors, shared, outs, name):
    whole = (TILE, RANK)
    return pl.pallas_call(
        kernel,
        grid=(4,),
        in_specs=[spec(whole)] * len(vectors) + [group(RANK, WIDE)] * 4 + [group(TILE, WIDE)] * 2,
        out_specs=[spec(whole)] * outs,
        out_shape=[shaped(*whole)] * outs,
        scratch_shapes=[pltpu.VMEM((2 * TILE, RANK), bf16)],
        compiler_params=params(),
        cost_estimate=cost(APPLY_COST, 6 << 20),
        name=name,
    )(*vectors, *shared)


def shift(value, axis, size, by):
    return lax.ppermute(value, axis, [(i, (i + by) % size) for i in range(size)])


def flip(value, axis, size, bit):
    return lax.ppermute(value, axis, [(i, i ^ bit) for i in range(size)])


def pick(value, index, axis=0):
    return lax.dynamic_index_in_dim(value, index, axis, keepdims=False)


VMEM = 16777216
REL = 1
FP = 'early'
TAIL = 'a2a'
XC = 0
NP = 'y'
XS = 'perm'
YS = 'perm'
DT = 'after'
CHUNKS = (56,8)


def everyone(value, axis, size):
    copies = jnp.broadcast_to(value[None], (size,) + value.shape)
    return lax.all_to_all(copies, axis, split_axis=0, concat_axis=0, tiled=True)


def along_y(value, move):
    pairs = [
        (s * 4 + r, move(s) * 4 + r) for s in range(4) for r in range(4) if s // 2 == r % 2
    ]
    return lax.ppermute(value, ("y", "rep"), pairs)


def per_device(factors_in, items, tile_user, levels):
    y, zh, x, core, rep = (lax.axis_index(name) for name in AXES)
    half, parity = rep // 2, rep % 2
    inside = y // 2 == parity
    strip = RANK // 4
    tie = lax.optimization_barrier

    copies = jnp.broadcast_to(items.T[None], (8, strip, TILE))
    copies, factors_in, tile_user = tie((copies, factors_in, tile_user))

    lev = levels[0].reshape(32, 2, HALF, TILE)
    other = pick(lev, 1 - half, 1)
    parts, at = [], 0
    for rows in CHUNKS:
        parts.append(other[:, at : at + rows])
        at += rows
    users = factors_in.T.reshape(strip, 2, TILE)
    kept = lax.dynamic_slice_in_dim(users, half * HALF, HALF, 2).reshape(strip, TILE)
    given = lax.dynamic_slice_in_dim(users, (1 - half) * HALF, HALF, 2).reshape(strip, TILE)
    blocks = jnp.zeros((8, TILE), f32).at[0, :32].set(tile_user[0].astype(f32))
    given = jnp.concatenate([given, blocks])

    moved_levels = []
    got = flip(given, "rep", 4, 2)
    low = jnp.where(half == 0, kept, got[:strip])
    high = jnp.where(half == 0, got[:strip], kept)
    pair = jnp.stack([low, high])
    next_pair = flip(pair, "rep", 4, 1)
    panel = lax.all_to_all(copies, ("zh", "rep"), split_axis=0, concat_axis=0, tiled=True)
    panel = panel.reshape(2, RANK, TILE)
    if NP == "z":
        panel, pair, next_pair, got, *parts = tie((panel, pair, next_pair, got, *parts))
    else:
        panel, pair, got, *parts = tie((panel, pair, got, *parts))
        next_pair = flip(pair, "rep", 4, 1)

    moved_levels.append(flip(parts[0], "rep", 4, 2))
    if YS == "perm":
        inside = y // 2 == parity
        beside = along_y(panel, lambda s: s ^ 1)
        across = along_y(panel, lambda s: 3 - s)
        beyond = along_y(panel, lambda s: (s + 2) % 4)
        same = jnp.where(inside, panel, beyond)
        odd = jnp.where(inside, beside, across)
        even = y % 2 == 0
        panel = jnp.stack([jnp.where(even, same, odd), jnp.where(even, odd, same)])
    elif YS == "two":
        inside = y // 2 == parity
        across = along_y(panel, lambda s: 3 - s)
        now = jnp.where(inside, panel, across)
        beside = flip(now, "y", 4, 1)
        even = (y % 2 == 0) == inside
        panel = jnp.stack([jnp.where(even, now, beside), jnp.where(even, beside, now)])
    else:
        panel = everyone(panel, "y", 4).reshape(4, 2, RANK, TILE)
        panel = lax.dynamic_slice_in_dim(panel, 2 * parity, 2, 0)
    panel = panel.reshape(4, RANK, TILE)
    panel, pair, got, *parts = tie((panel, pair, got, *parts[1:]))

    if XC:
        moved_levels.append(flip(parts[0], "rep", 4, 2))
        parts = parts[1:]
    if XS == "ring":
        left, right = shift(panel, "x", 4, 1), shift(panel, "x", 4, -1)
        over = jnp.concatenate([shift(left[:2], "x", 4, 1), shift(right[2:], "x", 4, -1)])
        own_panels = jnp.stack([panel, left, over, right])
    elif XS == "perm":
        own_panels = jnp.stack([panel] + [shift(panel, "x", 4, k) for k in (1, 2, 3)])
    else:
        own_panels = everyone(panel, "x", 4).reshape(4, 4, RANK, TILE)
    own_panels, pair, next_pair, got, moved_levels, *parts = tie(
        (own_panels, pair, next_pair, got, moved_levels, *parts)
    )
    moved_levels = moved_levels + [flip(rows, "rep", 4, 2) for rows in parts]
    far_panels = flip(own_panels, "core", 2, 1)
    user_b = got[strip, :32].astype(jnp.int32)
    place = jnp.stack([half, core, x]).astype(jnp.int32)
    scal = jnp.concatenate([place, tile_user[0], user_b])
    first = jnp.where(parity == 0, pair, next_pair)
    second = jnp.where(parity == 0, next_pair, pair)
    x0_t = jnp.stack([first, second], axis=1).reshape(RANK, TILE)

    *panels, own_scores, far_scores, x0 = first_scores(x0_t, own_panels, far_panels)
    *weights, target, far_target, part = first_apply(
        scal,
        (own_scores, far_scores),
        panels,
        lev.reshape(4, GROUPS, 2, HALF, TILE),
        [rows.reshape(4, GROUPS, -1, TILE) for rows in moved_levels],
    )
    shared = (*panels, *weights)
    part_b = flip(part, "rep", 4, 1)

    moved = [shift(jnp.stack([target[k], far_target[k]]), "x", 4, -k) for k in (1, 2, 3)]

    resid, part = next_apply(second_kernel, (part, part_b, x0), shared, 2, "second_apply")
    part_b = flip(part, "rep", 4, 1)
    x1, resid1, direc1, part = next_apply(
        third_kernel, (part, part_b, resid, x0), shared, 4, "third_apply"
    )
    part_b = flip(part, "rep", 4, 1)
    solved = pl.pallas_call(
        last_kernel,
        out_shape=shaped(TILE, RANK),
        compiler_params=params(),
        cost_estimate=cost(TILE * RANK * 10, 6 * TILE * RANK * 4),
        name="last_update",
    )(part, part_b, resid1, direc1, x1)

    vectors = [shift(solved, "x", 4, -k) for k in (1, 2, 3)]
    if DT == "after":
        vectors, moved = tie((vectors, moved))
    else:
        solved, moved = tie((solved, moved))
    got = flip(jnp.stack([far_target[0]] + [v[1] for v in moved]), "core", 2, 1)
    vectors = jnp.stack([solved] + vectors)
    far_vectors = flip(vectors, "core", 2, 1)

    vmem = pl.BlockSpec(memory_space=pltpu.VMEM)
    terms = pl.pallas_call(
        rhs_kernel,
        in_specs=[vmem] * 7,
        out_shape=shaped(2, 4, RANK, TILE),
        scratch_shapes=[pltpu.VMEM((RANK, WIDE), f32)],
        compiler_params=params(),
        cost_estimate=cost(4 * 1024 * RANK * WIDE, 4 << 20),
        name="rhs_terms",
    )(vectors, far_vectors, target, got, *moved)

    if FP == 'late':
        terms, solved = tie((terms, solved))
    strips = solved.reshape(TILE, 4, strip)
    sent = flip(pick(strips, rep ^ 2, 1), "rep", 4, 2)
    kept = pick(strips, rep, 1)
    low = jnp.where(half == 0, kept, sent).reshape(2, HALF, strip)
    high = jnp.where(half == 0, sent, kept).reshape(2, HALF, strip)
    factors = jnp.stack([low, high], axis=1).reshape(2 * TILE, strip)

    if TAIL == "one":
        pieces = lax.all_to_all(
            terms.reshape(32, strip, TILE),
            ("y", "zh", "rep"),
            split_axis=0,
            concat_axis=0,
            tiled=True,
        )
        pieces = pieces.reshape(4, 8, strip, TILE).sum(axis=0)
    else:
        if TAIL == "two":
            pair = terms.reshape(4, 8, strip, TILE)
            inside = y // 2 == parity
            mine = jnp.where(inside, 1 - y % 2, y % 2)
            kept_terms = pick(pair, 1 - mine)
            kept_terms = kept_terms + flip(pick(pair, mine), "y", 4, 1)
            pairs = [
                (s * 4 + r, (3 - s) * 4 + r)
                for s in range(4)
                for r in range(4)
                if s // 2 != r % 2
            ]
            summed = kept_terms + lax.ppermute(kept_terms, ("y", "rep"), pairs)
        else:
            summed = lax.all_to_all(
                terms.reshape(4, 8, strip, TILE), "y", split_axis=0, concat_axis=0, tiled=True
            ).sum(axis=0)
        summed, factors = tie((summed, factors))
        pieces = lax.all_to_all(
            summed, ("zh", "rep"), split_axis=0, concat_axis=0, tiled=True
        )
    chosen = pick(pieces.reshape(2, 2, 2, strip, TILE), y // 2, 2)
    scale = (2 * 64 * TILE) ** -0.5
    item_rhs = jnp.sum(chosen, axis=(0, 1)).T * (scale * STEP)
    return factors, item_rhs


def solution(mesh):
    fine = Mesh(np.asarray(mesh.devices).reshape(SIZES), AXES)
    rows = P(BLK, "rep")
    return jax.shard_map(
        per_device,
        mesh=fine,
        in_specs=(rows, rows, rows, P(BLK, "rep", None, None)),
        out_specs=(rows, rows),
        check_vma=False,
    )
```
